1024 devices in a mesh: dp: 128 (over x, y, core), blk: 8 (over z).
Axes of the slice: x: 8, y: 8, z: 8, core: 2. Of those that a mesh axis runs over, the one named last changes fastest.
Arguments:
- inputs: bfloat16 [1280, 8192], P(None, 'dp'), may hold values from -3 to 3
- grad_out: bfloat16 [1280, 8192], P(None, 'dp'), may hold values from -3 to 3
- up_weight: bfloat16 [8192, 28672], P('dp', 'blk'), may hold values from -0.0625 to 0.0625
- gate_weight: bfloat16 [8192, 28672], P('dp', 'blk'), may hold values from -0.0625 to 0.0625
- down_weight: bfloat16 [28672, 8192], P('blk', 'dp'), may hold values from -0.0625 to 0.0625
- saved_gate: bfloat16 [8, 30, 128, 128], P('blk'), may hold values from -6 to 6
- saved_up: bfloat16 [8, 30, 128, 128], P('blk'), may hold values from -6 to 6
- block_ids: int32 [10, 24], replicated, may hold values from 0 to 223, as said below
- counts: int32 [10], replicated, may hold values from 3 to 24, as said below
Outputs:
- grad_x: bfloat16 [1280, 8192], P('blk', 'dp')
- grad_w_up: bfloat16 [8192, 28672], P('dp', 'blk')
- grad_w_gate: bfloat16 [8192, 28672], P('dp', 'blk')
- grad_w_down: bfloat16 [28672, 8192], P('blk', 'dp')
The draws below stay inside these ranges and needn't reach their ends.
Inputs may be any that keep to these rules, and one draw needn't show every extreme that they name: `block_ids`: entries k < counts[t] of tile t's list are live and name distinct blocks; later entries are unused. The live entries of one tile name at most 3 blocks of any one owner (block b belongs to owner b // 28); over all tiles the live entries naming one owner's blocks number at most 30, and in every draw some owner reaches 30. `counts`: in every draw some tile has 24 live entries.
All inputs are finite; a program needn't handle non-finite values.
Results may differ from the reference program's by a relative error of at most 0.0057.
Values may be sent and summed in bfloat16 or wider, within the bound.
A program may use at most 32 MiB of HBM per device.

```python
import jax
import jax.numpy as jnp
from jax import lax

D = 8192
NB = 224
BLOCK = 128
TILE = 128
KMAX = 24
TILES = 10
FF = 28672
TOKENS = 1280
OWNERS = 8
OWN_BLOCKS = 28
PER_OWNER = 3
CAP = 30


def active_lists(key):
    hot_key, load_key, full_key, pick_key, order_key = jax.random.split(key, 5)
    hot_owner = jax.random.randint(hot_key, (), 0, OWNERS)
    full_tile = jax.random.randint(full_key, (), 0, TILES)
    owner_loads = jax.random.randint(load_key, (TILES, OWNERS), 0, PER_OWNER + 1)
    owner_range = jnp.arange(OWNERS, dtype=jnp.int32)
    tile_range = jnp.arange(TILES, dtype=jnp.int32)
    owner_loads = jnp.where((owner_range[None, :] == hot_owner) | (tile_range[:, None] == full_tile), PER_OWNER, owner_loads)
    scores = jax.random.randint(pick_key, (TILES, OWNERS, OWN_BLOCKS), 0, 1 << 20) * OWN_BLOCKS + jnp.arange(OWN_BLOCKS, dtype=jnp.int32)
    picked = jnp.argsort(scores, axis=-1)[:, :, :PER_OWNER].astype(jnp.int32)
    blocks = picked + (owner_range * OWN_BLOCKS)[None, :, None]
    used_entry = jnp.arange(PER_OWNER, dtype=jnp.int32)[None, None, :] < owner_loads[:, :, None]
    blocks = blocks.reshape(TILES, KMAX)
    used_entry = used_entry.reshape(TILES, KMAX)
    entry_range = jnp.arange(KMAX, dtype=jnp.int32)
    order_score = jax.random.randint(order_key, (TILES, KMAX), 0, 1 << 20) * KMAX + entry_range[None, :]
    order_score = jnp.where(used_entry, order_score, (1 << 26) + entry_range[None, :])
    arrangement = jnp.argsort(order_score, axis=-1)
    block_ids = jnp.take_along_axis(blocks, arrangement, axis=-1).astype(jnp.int32)
    counts = jnp.sum(owner_loads, axis=1).astype(jnp.int32)
    return (block_ids, counts)


def draw_block_ids(key, part):
    return active_lists(key)[0]


def draw_counts(key, part):
    return active_lists(key)[1]


def shard_levels(own_key, dims, pieces, smallest, top_value):
    level, own = 1.0, jax.random.fold_in(own_key, 6)
    for dim, blocks in pieces:
        steps = jnp.exp(jax.random.uniform(jax.random.fold_in(own, dim), (blocks,), jnp.float32, smallest / len(pieces), top_value / len(pieces)))
        level = level * jnp.repeat(steps, dims[dim] // blocks).reshape([-1 if axis == dim else 1 for axis in range(len(dims))])
    return level


def centred(stream_key, shape, width, limit, cuts=(), kind=jnp.bfloat16):
    result = width * jax.random.normal(stream_key, shape, jnp.float32)
    if cuts:
        result = result * shard_levels(stream_key, shape, cuts, -0.22, 0.18)
    return jnp.clip(result, -limit, limit).astype(kind)


def setup_inputs(seed: int = 0) -> dict:
    key_list = jax.random.split(jax.random.key(seed), 10)
    inputs = centred(key_list[0], (TOKENS, D), 0.5, 3.0, ((1, 128),))
    grad_out = centred(key_list[1], (TOKENS, D), 0.5, 3.0, ((1, 128),))
    up_weight = centred(key_list[2], (D, FF), D ** -0.5, 0.0625, ((0, 128), (1, 8)))
    gate_weight = centred(key_list[3], (D, FF), D ** -0.5, 0.0625, ((0, 128), (1, 8)))
    down_weight = centred(key_list[4], (FF, D), D ** -0.5, 0.0625, ((0, 8), (1, 128)))
    saved_gate = centred(key_list[5], (OWNERS, CAP, TILE, BLOCK), 1.0, 6.0, ((0, 8),))
    saved_up = centred(key_list[6], (OWNERS, CAP, TILE, BLOCK), 1.0, 6.0, ((0, 8),))
    block_ids = draw_block_ids(jax.random.fold_in(key_list[9], 71), 0)
    counts = draw_counts(jax.random.fold_in(key_list[9], 71), 0)
    return dict(inputs=inputs, grad_out=grad_out, up_weight=up_weight, gate_weight=gate_weight, down_weight=down_weight, saved_gate=saved_gate, saved_up=saved_up, block_ids=block_ids, counts=counts)


def compact(block_ids, counts, owner_index, own_blocks, capacity):
    tile_count = block_ids.shape[0]
    list_len = block_ids.shape[1]
    entries = jnp.arange(list_len, dtype=jnp.int32)
    live_entry = entries[None, :] < counts[:, None]
    owned_entry = (live_entry & (block_ids // own_blocks == owner_index)).reshape(-1).astype(jnp.int32)
    position = (jnp.cumsum(owned_entry) - 1).astype(jnp.int32)
    slot_index = jnp.arange(capacity, dtype=jnp.int32)
    matches = (owned_entry[None, :] == 1) & (position[None, :] == slot_index[:, None])
    pair_index = jnp.arange(tile_count * list_len, dtype=jnp.int32)
    chosen = jnp.sum(jnp.where(matches, pair_index[None, :], 0), axis=1).astype(jnp.int32)
    slot_live = jnp.sum(matches.astype(jnp.int32), axis=1).astype(jnp.int32)
    tile_of = (chosen // list_len).astype(jnp.int32)
    block_id = jnp.take(block_ids.reshape(-1), chosen).astype(jnp.int32)
    local_block = jnp.where(slot_live > 0, block_id - owner_index * own_blocks, 0).astype(jnp.int32)
    return tile_of, local_block, slot_live


def slot_grads(gate_in, up_in, slot_live, grad_hidden):
    gate_value = gate_in.astype(jnp.float32)
    up_value = up_in.astype(jnp.float32)
    mask_value = slot_live.astype(jnp.float32)[:, None, None]
    grad_value = grad_hidden.astype(jnp.float32)
    hidden = (jax.nn.relu(gate_value) * up_value * mask_value).astype(jnp.bfloat16)
    grad_gate = (grad_value * up_value * (gate_value > 0).astype(jnp.float32) * mask_value).astype(jnp.bfloat16)
    grad_up = (grad_value * jax.nn.relu(gate_value) * mask_value).astype(jnp.bfloat16)
    return hidden, grad_gate, grad_up


def reference(inputs, grad_out, up_weight, gate_weight, down_weight, saved_gate, saved_up, block_ids, counts):
    input_tiles = inputs.reshape(TILES, TILE, D)
    grad_tiles = grad_out.reshape(TILES, TILE, D)
    down_blocks = down_weight.reshape(NB, BLOCK, D)
    up_blocks = up_weight.reshape(D, NB, BLOCK)
    gate_blocks = gate_weight.reshape(D, NB, BLOCK)
    highest = lax.Precision.HIGHEST
    grad_total = jnp.zeros((TILES, TILE, D), jnp.float32)
    down_parts = []
    up_parts = []
    gate_parts = []
    for owner_index in range(OWNERS):
        tile_of, local_block, slot_live = compact(block_ids, counts, owner_index, OWN_BLOCKS, CAP)
        block_of = (local_block + owner_index * OWN_BLOCKS).astype(jnp.int32)
        input_slots = jnp.take(input_tiles, tile_of, axis=0).astype(jnp.float32)
        grad_slots = jnp.take(grad_tiles, tile_of, axis=0).astype(jnp.float32)
        down_slots = jnp.take(down_blocks, block_of, axis=0).astype(jnp.float32)
        up_slots = jnp.take(up_blocks, block_of, axis=1).astype(jnp.float32)
        gate_slots = jnp.take(gate_blocks, block_of, axis=1).astype(jnp.float32)
        grad_hidden = jnp.einsum('std,sbd->stb', grad_slots, down_slots, precision=highest).astype(jnp.bfloat16)
        hidden, grad_gate, grad_up = slot_grads(saved_gate[owner_index], saved_up[owner_index], slot_live, grad_hidden)
        owned_block = ((local_block[:, None] == jnp.arange(OWN_BLOCKS, dtype=jnp.int32)[None, :]) & (slot_live[:, None] > 0)).astype(jnp.float32)
        down_terms = jnp.einsum('stb,std->sbd', hidden.astype(jnp.float32), grad_slots, precision=highest)
        down_sum = jnp.einsum('so,sbd->obd', owned_block, down_terms, precision=highest)
        down_parts.append(down_sum.reshape(OWN_BLOCKS * BLOCK, D).astype(jnp.bfloat16))
        up_terms = jnp.einsum('std,stb->sdb', input_slots, grad_up.astype(jnp.float32), precision=highest)
        up_sum = jnp.einsum('so,sdb->dob', owned_block, up_terms, precision=highest)
        up_parts.append(up_sum.reshape(D, OWN_BLOCKS * BLOCK).astype(jnp.bfloat16))
        gate_terms = jnp.einsum('std,stb->sdb', input_slots, grad_gate.astype(jnp.float32), precision=highest)
        gate_sum = jnp.einsum('so,sdb->dob', owned_block, gate_terms, precision=highest)
        gate_parts.append(gate_sum.reshape(D, OWN_BLOCKS * BLOCK).astype(jnp.bfloat16))
        input_terms = jnp.einsum('stb,dsb->std', grad_gate.astype(jnp.float32), gate_slots, precision=highest)
        input_terms = input_terms + jnp.einsum('stb,dsb->std', grad_up.astype(jnp.float32), up_slots, precision=highest)
        tile_match = ((tile_of[:, None] == jnp.arange(TILES, dtype=jnp.int32)[None, :]) & (slot_live[:, None] > 0)).astype(jnp.float32)
        grad_total = grad_total + jnp.einsum('sn,std->ntd', tile_match, input_terms, precision=highest)
    grad_x = grad_total.reshape(TOKENS, D).astype(jnp.bfloat16)
    grad_w_up = jnp.concatenate(up_parts, axis=1)
    grad_w_gate = jnp.concatenate(gate_parts, axis=1)
    grad_w_down = jnp.concatenate(down_parts, axis=0)
    return (grad_x, grad_w_up, grad_w_gate, grad_w_down)
```

```python
import functools

import jax
import jax.numpy as jnp
from jax import lax
from jax.experimental import pallas as pl
from jax.experimental.pallas import tpu as pltpu
from jax.sharding import PartitionSpec as P

MESH = pl.DeviceIdType.MESH
BF16 = jnp.bfloat16
F32 = jnp.float32

WIDTH = 64
TILES = 10
TILE = 128
BLOCK = 128
KMAX = 24
PER = 3
PAIRS = TILES * PER
OWN = 28
HALF_PAIRS = PAIRS // 2
HALF_TILES = TILES // 2
HALF = HALF_PAIRS * TILE
PART_ROWS = WIDTH + 16
VMEM_LIMIT = 24 * 1024 * 1024


def sizes(side):
    chunk = HALF // side
    return chunk, -(-chunk // side // 16) * 16


def rows_of(ref, half, place, chunk, stride):
    first = place * TILE
    parts = []
    left = TILE
    while left:
        number, offset = divmod(first, chunk)
        take = min(left, chunk - offset)
        start = number * stride + offset
        parts.append(ref[half, start : start + take, :])
        first += take
        left -= take
    return parts[0] if len(parts) == 1 else jnp.concatenate(parts, axis=0)


def terms_kernel(ids, counts, go, down, own, half_send, places):
    core = lax.rem(lax.axis_index("dp"), 2)
    low = lax.axis_index("blk") * OWN

    def scan_tile(t, first):
        live = counts[t]
        packed = jnp.int32(0)
        scale = jnp.int32(1)
        number = jnp.int32(0)
        for k in range(KMAX):
            block = ids[t, k] - low
            owned = (block >= 0) & (block < OWN) & (live > k)
            packed = packed + jnp.where(owned, (block + 1) * scale, 0)
            scale = jnp.where(owned, scale * 32, scale)
            number = number + jnp.where(owned, 1, 0)
        for j in range(PER):
            places[t * PER + j] = lax.shift_right_logical(packed, jnp.int32(5 * j)) & 31
            places[PAIRS + t * PER + j] = jnp.minimum(first + j, PAIRS - 1)
        return first + number

    lax.fori_loop(0, TILES, scan_tile, jnp.int32(0))

    def hidden_terms(t):
        tokens = go[:, pl.ds(pl.multiple_of(t * TILE, TILE), TILE)]
        blocks = []
        for j in range(PER):
            block = jnp.maximum(places[t * PER + j] - 1, 0)
            blocks.append(down[:, pl.ds(pl.multiple_of(block * BLOCK, BLOCK), BLOCK)])
        weights = jnp.concatenate(blocks, axis=1)
        return lax.dot_general(
            tokens, weights, (((0,), (0,)), ((), ())), preferred_element_type=F32
        )

    for i in range(HALF_TILES):
        others = hidden_terms((1 - core) * HALF_TILES + i)
        mine = hidden_terms(core * HALF_TILES + i)
        for j in range(PER):
            start = (i * PER + j) * TILE
            columns = slice(j * BLOCK, (j + 1) * BLOCK)
            half_send[start : start + TILE, :] = others[:, columns].astype(BF16)
            own[start : start + TILE, :] = mine[:, columns]


def sum_kernel(
    side,
    own_hbm,
    half_send,
    gh,
    own,
    half_recv,
    a_send,
    a_recv,
    b_send,
    b_recv,
    load_sem,
    h_ssem,
    h_rsem,
    a_ssem,
    a_rsem,
    b_ssem,
    b_rsem,
    c_ssem,
    c_rsem,
    d_ssem,
    d_rsem,
    f_ssem,
    f_rsem,
):
    chunk, piece = sizes(side)
    stride = piece * side
    dp = lax.axis_index("dp")
    me_z = lax.axis_index("blk")
    core = dp % 2
    me_y = (dp // 2) % side
    me_x = dp // (2 * side)
    partner = dp + 1 - 2 * core
    me_a = me_x + core * (me_y - me_x)
    me_b = me_y + core * (me_x - me_y)
    step_a = (1 - core) * 2 * side + core * 2
    step_b = (1 - core) * 2 + core * 2 * side

    def along_a(i):
        return dp + (i - me_a) * step_a

    def along_b(i):
        return dp + (i - me_b) * step_b

    def other(me, d):
        return (me + d) % side

    load = pltpu.make_async_copy(own_hbm, own, load_sem)
    load.start()

    barrier = pltpu.get_barrier_semaphore()
    pl.semaphore_signal(barrier, inc=1, device_id=(partner, me_z), device_id_type=MESH)
    for d in range(1, side):
        pl.semaphore_signal(
            barrier, inc=1, device_id=(along_a(other(me_a, d)), me_z), device_id_type=MESH
        )
        pl.semaphore_signal(
            barrier, inc=1, device_id=(along_b(other(me_b, d)), me_z), device_id_type=MESH
        )
    pl.semaphore_wait(barrier, 1 + 2 * (side - 1))

    def h_copy():
        return pltpu.make_async_remote_copy(
            src_ref=half_send,
            dst_ref=half_recv,
            send_sem=h_ssem,
            recv_sem=h_rsem,
            device_id=(partner, me_z),
            device_id_type=MESH,
        )

    h_copy().start()
    load.wait()
    h_copy().wait_recv()
    for i in range(HALF_TILES):
        rows = slice(i * PER * TILE, (i + 1) * PER * TILE)
        a_send[rows, :] = (own[rows, :] + half_recv[rows, :].astype(F32)).astype(BF16)

    def chunk_rows(i):
        return pl.ds(pl.multiple_of(i * chunk, 16), chunk)

    def a_copy(to, slot):
        return pltpu.make_async_remote_copy(
            src_ref=a_send.at[chunk_rows(to)],
            dst_ref=a_recv.at[slot],
            send_sem=a_ssem.at[to],
            recv_sem=a_rsem.at[slot],
            device_id=(along_a(to), me_z),
            device_id_type=MESH,
        )

    order = sorted(range(1, side), key=lambda d: -min(d, side - d))
    for d in order:
        a_copy(other(me_a, d), me_a).start()
    total = a_send[chunk_rows(me_a), :].astype(F32)
    for d in reversed(order):
        source = other(me_a, d)
        a_copy(source, source).wait_recv()
        total = total + a_recv[source].astype(F32)
    b_send[0:chunk, :] = total.astype(BF16)
    if stride > chunk:
        b_send[chunk:stride, :] = jnp.zeros((stride - chunk, BLOCK), BF16)

    def piece_rows(i):
        return pl.ds(pl.multiple_of(i * piece, 16), piece)

    def b_copy(to, slot):
        return pltpu.make_async_remote_copy(
            src_ref=b_send.at[piece_rows(to)],
            dst_ref=b_recv.at[slot],
            send_sem=b_ssem.at[to],
            recv_sem=b_rsem.at[slot],
            device_id=(along_b(to), me_z),
            device_id_type=MESH,
        )

    for d in order:
        b_copy(other(me_b, d), me_b).start()
    total = b_send[piece_rows(me_b), :].astype(F32)
    for d in reversed(order):
        source = other(me_b, d)
        b_copy(source, source).wait_recv()
        total = total + b_recv[source].astype(F32)

    def c_copy(to, slot):
        rows = pl.ds(pl.multiple_of(me_a * stride + slot * piece, 16), piece)
        return pltpu.make_async_remote_copy(
            src_ref=gh.at[core, rows],
            dst_ref=gh.at[core, rows],
            send_sem=c_ssem.at[to],
            recv_sem=c_rsem.at[slot],
            device_id=(along_b(to), me_z),
            device_id_type=MESH,
        )

    def d_copy(to, slot):
        rows = pl.ds(pl.multiple_of(slot * stride, 16), chunk)
        return pltpu.make_async_remote_copy(
            src_ref=gh.at[core, rows],
            dst_ref=gh.at[core, rows],
            send_sem=d_ssem.at[to],
            recv_sem=d_rsem.at[slot],
            device_id=(along_a(to), me_z),
            device_id_type=MESH,
        )

    def f_copy(slot, half):
        rows = pl.ds(pl.multiple_of(slot * stride, 16), chunk)
        return pltpu.make_async_remote_copy(
            src_ref=gh.at[half, rows],
            dst_ref=gh.at[half, rows],
            send_sem=f_ssem.at[slot],
            recv_sem=f_rsem.at[slot],
            device_id=(partner, me_z),
            device_id_type=MESH,
        )

    rows = pl.ds(pl.multiple_of(me_a * stride + me_b * piece, 16), piece)
    gh[core, rows, :] = total.astype(BF16)
    for d in order:
        c_copy(other(me_b, d), me_b).start()
    for d in reversed(order):
        source = other(me_b, d)
        c_copy(source, source).wait_recv()
    for d in order:
        d_copy(other(me_a, d), me_a).start()
    f_copy(me_a, core).start()
    for d in reversed(order):
        source = other(me_a, d)
        d_copy(source, source).wait_recv()
        f_copy(source, core).start()
    for d in range(side):
        f_copy(d, 1 - core).wait_recv()

    h_copy().wait_send()
    for d in range(1, side):
        a_copy(other(me_a, d), me_a).wait_send()
        b_copy(other(me_b, d), me_b).wait_send()
        c_copy(other(me_b, d), me_b).wait_send()
        d_copy(other(me_a, d), me_a).wait_send()
    for d in range(side):
        f_copy(d, core).wait_send()


def grads_kernel(
    side,
    depth,
    places,
    gh,
    go,
    inp,
    up,
    gate,
    sg,
    su,
    up_out,
    gate_out,
    down_out,
    parts,
    totals,
    gx,
):
    chunk, piece = sizes(side)
    stride = piece * side
    totals[...] = jnp.zeros_like(totals)
    for t in range(TILES):
        half, i = divmod(t, HALF_TILES)
        weights = []
        values = []
        tokens = slice(t * TILE, (t + 1) * TILE)
        for j in range(PER):
            number = t * PER + j
            place = places[number]
            slot = places[PAIRS + number]
            live = jnp.where(place > 0, jnp.float32(1), jnp.float32(0))
            block = jnp.maximum(place - 1, 0)
            gate_value = sg[slot].astype(F32)
            up_value = su[slot].astype(F32)
            positive = jnp.maximum(gate_value, 0.0) * live
            value = rows_of(gh, half, i * PER + j, chunk, stride).astype(F32)
            hidden = (positive * up_value).astype(BF16)
            grad_up = (value * positive).astype(BF16)
            grad_gate = (value * (jnp.where(gate_value > 0, up_value, 0.0) * live)).astype(BF16)
            columns = pl.ds(pl.multiple_of(block * BLOCK, BLOCK), BLOCK)
            weights += [up[:, columns], gate[:, columns]]
            values += [grad_up, grad_gate]
            pair = jnp.dot(
                inp[:, tokens],
                jnp.concatenate([grad_up, grad_gate], axis=1),
                preferred_element_type=F32,
            )
            totals[0, block] += pair[:, 0:BLOCK]
            totals[1, block] += pair[:, BLOCK : 2 * BLOCK]
            totals[2, block] += jnp.dot(go[:, tokens], hidden, preferred_element_type=F32)
        gx[t] = lax.dot_general(
            jnp.concatenate(weights, axis=1),
            jnp.concatenate(values, axis=1),
            (((1,), (1,)), ((), ())),
            preferred_element_type=F32,
        )
    for i, out in enumerate((up_out, gate_out, down_out)):
        for b in range(OWN):
            out[:, b * BLOCK : (b + 1) * BLOCK] = totals[i, b].astype(BF16)

    lanes = lax.broadcasted_iota(jnp.int32, (WIDTH, TILE), 1)
    short = lax.broadcasted_iota(jnp.int32, (16, TILE), 1)
    for to in range(depth):
        q, o = divmod(to * TILES * TILE // depth, TILE)
        after = gx[q + 1]
        if o:
            first = jnp.where(
                lanes < TILE - o,
                pltpu.roll(gx[q], TILE - o, 1),
                pltpu.roll(after, TILE - o, 1),
            )
        else:
            first = gx[q]
        parts[to, 0:WIDTH, :] = first.astype(BF16)
        rest = jnp.zeros((16, TILE), F32)
        for s in range(4):
            shift = (32 * s - o) % TILE
            moved = after[16 * s : 16 * (s + 1), :]
            if shift:
                moved = pltpu.roll(moved, shift, 1)
            rest = jnp.where(short // 32 == s, moved, rest)
        parts[to, WIDTH:PART_ROWS, :] = rest.astype(BF16)


def parts_kernel(depth, parts, gx_out, own, recv, load_sem, ssem, rsem):
    dp = lax.axis_index("dp")
    me_z = lax.axis_index("blk")
    load = pltpu.make_async_copy(parts.at[me_z], own, load_sem)
    load.start()

    def other(d):
        return (me_z + d) % depth

    barrier = pltpu.get_barrier_semaphore()
    for d in range(1, depth):
        pl.semaphore_signal(barrier, inc=1, device_id=(dp, other(d)), device_id_type=MESH)
    pl.semaphore_wait(barrier, depth - 1)

    def z_copy(to, slot):
        return pltpu.make_async_remote_copy(
            src_ref=parts.at[to],
            dst_ref=recv.at[slot],
            send_sem=ssem.at[to],
            recv_sem=rsem.at[slot],
            device_id=(dp, to),
            device_id_type=MESH,
        )

    order = sorted(range(1, depth), key=lambda d: -min(d, depth - d))
    for d in order:
        z_copy(other(d), me_z).start()
    load.wait()
    total = own[...].astype(F32)
    for d in reversed(order):
        source = other(d)
        z_copy(source, source).wait_recv()
        total = total + recv[source].astype(F32)
    gx_out[:, 0:TILE] = total[0:WIDTH, :].astype(BF16)
    rest = total[WIDTH:PART_ROWS, :]
    for s in range(4):
        moved = pltpu.roll(rest, TILE - 32 * s, 1) if s else rest
        gx_out[16 * s : 16 * (s + 1), TILE : TILE + 32] = moved[:, 0:32].astype(BF16)
    for d in range(1, depth):
        z_copy(other(d), me_z).wait_send()


def shards(
    side,
    depth,
    inputs,
    grad_out,
    up_weight,
    gate_weight,
    down_weight,
    saved_gate,
    saved_up,
    block_ids,
    counts,
):
    tokens = TILES * TILE
    units = OWN * BLOCK
    chunk, piece = sizes(side)
    stride = piece * side
    dma = pltpu.SemaphoreType.DMA
    anywhere = pl.BlockSpec(memory_space=pl.ANY)
    smem = pl.BlockSpec(memory_space=pltpu.SMEM)
    vmem = pl.BlockSpec(memory_space=pltpu.VMEM)
    go = grad_out.T
    shape = jax.ShapeDtypeStruct
    own, half_send, places = pl.pallas_call(
        terms_kernel,
        out_shape=[
            shape((HALF, BLOCK), F32),
            shape((HALF, BLOCK), BF16),
            shape((2 * PAIRS,), jnp.int32),
        ],
        in_specs=[smem, smem, vmem, vmem],
        out_specs=[vmem, vmem, smem],
        compiler_params=pltpu.CompilerParams(vmem_limit_bytes=VMEM_LIMIT),
    )(block_ids, counts, go, down_weight.T)
    gh = pl.pallas_call(
        functools.partial(sum_kernel, side),
        out_shape=shape((2, side * stride, BLOCK), BF16),
        in_specs=[anywhere, anywhere],
        out_specs=vmem,
        scratch_shapes=[
            pltpu.VMEM((HALF, BLOCK), F32),
            pltpu.VMEM((HALF, BLOCK), BF16),
            pltpu.VMEM((HALF, BLOCK), BF16),
            pltpu.VMEM((side, chunk, BLOCK), BF16),
            pltpu.VMEM((stride, BLOCK), BF16),
            pltpu.VMEM((side, piece, BLOCK), BF16),
            dma,
            dma,
            dma,
        ]
        + [dma((side,))] * 10,
        compiler_params=pltpu.CompilerParams(
            collective_id=0, has_side_effects=True, vmem_limit_bytes=VMEM_LIMIT
        ),
    )(own, half_send)
    grad_up, grad_gate, grad_down, parts = pl.pallas_call(
        functools.partial(grads_kernel, side, depth),
        out_shape=[shape((WIDTH, units), BF16)] * 3
        + [shape((depth, PART_ROWS, TILE), BF16)],
        in_specs=[smem] + [vmem] * 7,
        out_specs=[vmem] * 4,
        scratch_shapes=[
            pltpu.VMEM((3, OWN, WIDTH, BLOCK), F32),
            pltpu.VMEM((TILES, WIDTH, TILE), F32),
        ],
        compiler_params=pltpu.CompilerParams(vmem_limit_bytes=VMEM_LIMIT),
    )(places, gh, go, inputs.T, up_weight, gate_weight, saved_gate[0], saved_up[0])
    grad_x = pl.pallas_call(
        functools.partial(parts_kernel, depth),
        out_shape=shape((WIDTH, tokens // depth), BF16),
        in_specs=[anywhere],
        out_specs=vmem,
        scratch_shapes=[
            pltpu.VMEM((PART_ROWS, TILE), BF16),
            pltpu.VMEM((depth, PART_ROWS, TILE), BF16),
            dma,
            dma((depth,)),
            dma((depth,)),
        ],
        compiler_params=pltpu.CompilerParams(
            collective_id=1, has_side_effects=True, vmem_limit_bytes=VMEM_LIMIT
        ),
    )(parts)
    return (grad_x.T, grad_up, grad_gate, grad_down.T)


def solution(mesh):
    side = 1
    while 2 * side * side < mesh.shape["dp"]:
        side += 1
    in_specs = (
        P(None, "dp"),
        P(None, "dp"),
        P("dp", "blk"),
        P("dp", "blk"),
        P("blk", "dp"),
        P("blk", None, None, None),
        P("blk", None, None, None),
        P(),
        P(),
    )
    out_specs = (P("blk", "dp"), P("dp", "blk"), P("dp", "blk"), P("blk", "dp"))
    return jax.shard_map(
        functools.partial(shards, side, mesh.shape["blk"]),
        mesh=mesh,
        in_specs=in_specs,
        out_specs=out_specs,
        check_vma=False,
    )
```

```python
import functools

import jax
import jax.numpy as jnp
from jax import lax
from jax.experimental import pallas as pl
from jax.experimental.pallas import tpu as pltpu
from jax.sharding import PartitionSpec as P

MESH = pl.DeviceIdType.MESH
BF16 = jnp.bfloat16
F32 = jnp.float32

WIDTH = 64
TILES = 10
TILE = 128
BLOCK = 128
KMAX = 24
PER = 3
PAIRS = TILES * PER
OWN = 28
HALF_PAIRS = PAIRS // 2
HALF_TILES = TILES // 2
HALF = HALF_PAIRS * TILE
PART_ROWS = WIDTH + 16
VMEM_LIMIT = 24 * 1024 * 1024


EARLY = 1
SUBS = 2


def sizes(side):
    chunk = HALF // side
    subs = []
    offset = 0
    for n in range(SUBS):
        number = min(-(-chunk // (SUBS * 16 * side)) * 16 * side, chunk - offset)
        piece = -(-number // side // 16) * 16
        subs.append((offset, number, piece))
        offset += number
    return chunk, subs


def stride_of(side):
    return sum(piece for _, _, piece in sizes(side)[1]) * side


def rows_of(ref, half, place, chunk, stride):
    first = place * TILE
    parts = []
    left = TILE
    while left:
        number, offset = divmod(first, chunk)
        take = min(left, chunk - offset)
        start = number * stride + offset
        parts.append(ref[half, start : start + take, :])
        first += take
        left -= take
    return parts[0] if len(parts) == 1 else jnp.concatenate(parts, axis=0)


def pick_kernel(ids, counts, down_hbm, picked, places, down, load_sem):
    load = pltpu.make_async_copy(down_hbm, down, load_sem)
    load.start()
    low = lax.axis_index("blk") * OWN

    first = jnp.int32(0)
    for t in range(TILES):
        live = counts[t]
        packed = jnp.int32(0)
        shift = jnp.int32(0)
        for k in range(KMAX):
            block = ids[t, k] - low
            owned = (block >= 0) & (block < OWN) & (live > k)
            packed = packed + jnp.where(owned, lax.shift_left(block + 1, shift), 0)
            shift = shift + jnp.where(owned, 5, 0)
        number = jnp.int32(0)
        for j in range(PER):
            place = lax.shift_right_logical(packed, jnp.int32(5 * j)) & 31
            places[t * PER + j] = place
            places[PAIRS + t * PER + j] = jnp.minimum(first + j, PAIRS - 1)
            number = number + jnp.where(place > 0, 1, 0)
        first = first + number

    load.wait()
    for t in range(TILES):
        for j in range(PER):
            block = jnp.maximum(places[t * PER + j] - 1, 0)
            columns = pl.ds(pl.multiple_of(block * BLOCK, BLOCK), BLOCK)
            picked[t, :, j * BLOCK : (j + 1) * BLOCK] = down[:, columns]


def sum_kernel(
    side,
    go,
    picked,
    inp_hbm,
    up_hbm,
    gate_hbm,
    sg_hbm,
    su_hbm,
    gh,
    inp,
    up,
    gate,
    sg,
    su,
    own,
    half_send,
    half_recv,
    a_send,
    a_recv,
    b_send,
    b_recv,
    load_sem,
    h_ssem,
    h_rsem,
    a_ssem,
    a_rsem,
    b_ssem,
    b_rsem,
    c_ssem,
    c_rsem,
    d_ssem,
    d_rsem,
    f_ssem,
    f_rsem,
):
    chunk, subs = sizes(side)
    stride = stride_of(side)
    dp = lax.axis_index("dp")
    me_z = lax.axis_index("blk")
    core = dp % 2
    me_y = (dp // 2) % side
    me_x = dp // (2 * side)
    partner = dp + 1 - 2 * core
    me_a = me_x + core * (me_y - me_x)
    me_b = me_y + core * (me_x - me_y)
    step_a = (1 - core) * 2 * side + core * 2
    step_b = (1 - core) * 2 + core * 2 * side

    def along_a(i):
        return dp + (i - me_a) * step_a

    def along_b(i):
        return dp + (i - me_b) * step_b

    def other(me, d):
        return (me + d) % side

    barrier = pltpu.get_barrier_semaphore()
    pl.semaphore_signal(barrier, inc=1, device_id=(partner, me_z), device_id_type=MESH)
    for d in range(1, side):
        pl.semaphore_signal(
            barrier, inc=1, device_id=(along_a(other(me_a, d)), me_z), device_id_type=MESH
        )
        pl.semaphore_signal(
            barrier, inc=1, device_id=(along_b(other(me_b, d)), me_z), device_id_type=MESH
        )

    loads = [
        pltpu.make_async_copy(source, target, load_sem.at[i])
        for i, (source, target) in enumerate(
            ((inp_hbm, inp), (up_hbm, up), (gate_hbm, gate), (sg_hbm, sg), (su_hbm, su))
        )
    ]
    for load in loads:
        load.start()

    def hidden_terms(t):
        tokens = go[:, pl.ds(pl.multiple_of(t * TILE, TILE), TILE)]
        return lax.dot_general(
            tokens, picked[t], (((0,), (0,)), ((), ())), preferred_element_type=F32
        )

    def h_copy(i):
        rows = pl.ds(i * PER * TILE, PER * TILE)
        return pltpu.make_async_remote_copy(
            src_ref=half_send.at[rows],
            dst_ref=half_recv.at[rows],
            send_sem=h_ssem.at[i],
            recv_sem=h_rsem.at[i],
            device_id=(partner, me_z),
            device_id_type=MESH,
        )

    for i in range(HALF_TILES):
        others = hidden_terms((1 - core) * HALF_TILES + i)
        for j in range(PER):
            start = (i * PER + j) * TILE
            half_send[start : start + TILE, :] = others[:, j * BLOCK : (j + 1) * BLOCK].astype(BF16)
    for i in range(HALF_TILES):
        mine = hidden_terms(core * HALF_TILES + i)
        for j in range(PER):
            start = (i * PER + j) * TILE
            own[start : start + TILE, :] = mine[:, j * BLOCK : (j + 1) * BLOCK]
        if i == EARLY:
            pl.semaphore_wait(barrier, 1 + 2 * (side - 1))
            for k in range(HALF_TILES):
                h_copy(k).start()
    for i in range(HALF_TILES):
        h_copy(i).wait_recv()
        rows = slice(i * PER * TILE, (i + 1) * PER * TILE)
        a_send[rows, :] = (own[rows, :] + half_recv[rows, :].astype(F32)).astype(BF16)

    def a_copy(to, slot, n):
        offset, number, _ = subs[n]
        rows = pl.ds(pl.multiple_of(to * chunk + offset, 16), number)
        return pltpu.make_async_remote_copy(
            src_ref=a_send.at[rows],
            dst_ref=a_recv.at[slot, offset : offset + number],
            send_sem=a_ssem.at[n, to],
            recv_sem=a_rsem.at[n, slot],
            device_id=(along_a(to), me_z),
            device_id_type=MESH,
        )

    def b_copy(to, slot, n):
        offset, _, piece = subs[n]
        rows = pl.ds(pl.multiple_of(offset + to * piece, 16), piece)
        return pltpu.make_async_remote_copy(
            src_ref=b_send.at[rows],
            dst_ref=b_recv.at[n, slot, 0:piece],
            send_sem=b_ssem.at[n, to],
            recv_sem=b_rsem.at[n, slot],
            device_id=(along_b(to), me_z),
            device_id_type=MESH,
        )

    def c_copy(to, slot, n):
        offset, _, piece = subs[n]
        rows = pl.ds(pl.multiple_of(me_a * stride + offset + slot * piece, 16), piece)
        return pltpu.make_async_remote_copy(
            src_ref=gh.at[core, rows],
            dst_ref=gh.at[core, rows],
            send_sem=c_ssem.at[n, to],
            recv_sem=c_rsem.at[n, slot],
            device_id=(along_b(to), me_z),
            device_id_type=MESH,
        )

    def d_copy(to, slot, n):
        offset, number, _ = subs[n]
        rows = pl.ds(pl.multiple_of(slot * stride + offset, 16), number)
        return pltpu.make_async_remote_copy(
            src_ref=gh.at[core, rows],
            dst_ref=gh.at[core, rows],
            send_sem=d_ssem.at[n, to],
            recv_sem=d_rsem.at[n, slot],
            device_id=(along_a(to), me_z),
            device_id_type=MESH,
        )

    def f_copy(slot, half, n):
        offset, number, _ = subs[n]
        rows = pl.ds(pl.multiple_of(slot * stride + offset, 16), number)
        return pltpu.make_async_remote_copy(
            src_ref=gh.at[half, rows],
            dst_ref=gh.at[half, rows],
            send_sem=f_ssem.at[n, slot],
            recv_sem=f_rsem.at[n, slot],
            device_id=(partner, me_z),
            device_id_type=MESH,
        )

    order = sorted(range(1, side), key=lambda d: -min(d, side - d))
    steps = range(len(subs))
    for n in steps:
        for d in order:
            a_copy(other(me_a, d), me_a, n).start()
    for n in steps:
        offset, number, piece = subs[n]
        rows = pl.ds(pl.multiple_of(me_a * chunk + offset, 16), number)
        total = a_send[rows, :].astype(F32)
        for d in reversed(order):
            source = other(me_a, d)
            a_copy(source, source, n).wait_recv()
            total = total + a_recv[source, offset : offset + number, :].astype(F32)
        b_send[offset : offset + number, :] = total.astype(BF16)
        end = offset + piece * side
        if end > offset + number:
            b_send[offset + number : end, :] = jnp.zeros((end - offset - number, BLOCK), BF16)
        for d in order:
            b_copy(other(me_b, d), me_b, n).start()
    for n in steps:
        offset, _, piece = subs[n]
        total = b_send[pl.ds(pl.multiple_of(offset + me_b * piece, 16), piece), :].astype(F32)
        for d in reversed(order):
            source = other(me_b, d)
            b_copy(source, source, n).wait_recv()
            total = total + b_recv[n, source, 0:piece, :].astype(F32)
        rows = pl.ds(pl.multiple_of(me_a * stride + offset + me_b * piece, 16), piece)
        gh[core, rows, :] = total.astype(BF16)
        for d in order:
            c_copy(other(me_b, d), me_b, n).start()
    for n in steps:
        for d in reversed(order):
            source = other(me_b, d)
            c_copy(source, source, n).wait_recv()
        for d in order:
            d_copy(other(me_a, d), me_a, n).start()
        f_copy(me_a, core, n).start()
    for n in steps:
        for d in reversed(order):
            source = other(me_a, d)
            d_copy(source, source, n).wait_recv()
            f_copy(source, core, n).start()
    for n in steps:
        for d in range(side):
            f_copy(d, 1 - core, n).wait_recv()

    for load in loads:
        load.wait()
    for i in range(HALF_TILES):
        h_copy(i).wait_send()
    for n in steps:
        for d in range(1, side):
            a_copy(other(me_a, d), me_a, n).wait_send()
            b_copy(other(me_b, d), me_b, n).wait_send()
            c_copy(other(me_b, d), me_b, n).wait_send()
            d_copy(other(me_a, d), me_a, n).wait_send()
        for d in range(side):
            f_copy(d, core, n).wait_send()


def grads_kernel(
    side,
    depth,
    places,
    gh,
    go,
    inp,
    up,
    gate,
    sg,
    su,
    up_out,
    gate_out,
    down_out,
    parts,
    totals,
    gx,
):
    chunk, _ = sizes(side)
    stride = stride_of(side)
    totals[...] = jnp.zeros_like(totals)
    for t in range(TILES):
        half, i = divmod(t, HALF_TILES)
        weights = []
        values = []
        tokens = slice(t * TILE, (t + 1) * TILE)
        for j in range(PER):
            number = t * PER + j
            place = places[number]
            slot = places[PAIRS + number]
            live = jnp.where(place > 0, jnp.float32(1), jnp.float32(0))
            block = jnp.maximum(place - 1, 0)
            gate_value = sg[slot].astype(F32)
            up_value = su[slot].astype(F32)
            positive = jnp.maximum(gate_value, 0.0) * live
            value = rows_of(gh, half, i * PER + j, chunk, stride).astype(F32)
            hidden = (positive * up_value).astype(BF16)
            grad_up = (value * positive).astype(BF16)
            grad_gate = (value * (jnp.where(gate_value > 0, up_value, 0.0) * live)).astype(BF16)
            columns = pl.ds(pl.multiple_of(block * BLOCK, BLOCK), BLOCK)
            weights += [up[:, columns], gate[:, columns]]
            values += [grad_up, grad_gate]
            pair = jnp.dot(
                inp[:, tokens],
                jnp.concatenate([grad_up, grad_gate], axis=1),
                preferred_element_type=F32,
            )
            totals[0, block] += pair[:, 0:BLOCK]
            totals[1, block] += pair[:, BLOCK : 2 * BLOCK]
            totals[2, block] += jnp.dot(go[:, tokens], hidden, preferred_element_type=F32)
        gx[t] = lax.dot_general(
            jnp.concatenate(weights, axis=1),
            jnp.concatenate(values, axis=1),
            (((1,), (1,)), ((), ())),
            preferred_element_type=F32,
        )
    for i, out in enumerate((up_out, gate_out, down_out)):
        for b in range(OWN):
            out[:, b * BLOCK : (b + 1) * BLOCK] = totals[i, b].astype(BF16)

    lanes = lax.broadcasted_iota(jnp.int32, (WIDTH, TILE), 1)
    short = lax.broadcasted_iota(jnp.int32, (16, TILE), 1)
    for to in range(depth):
        q, o = divmod(to * TILES * TILE // depth, TILE)
        after = gx[q + 1]
        if o:
            first = jnp.where(
                lanes < TILE - o,
                pltpu.roll(gx[q], TILE - o, 1),
                pltpu.roll(after, TILE - o, 1),
            )
        else:
            first = gx[q]
        parts[to, 0:WIDTH, :] = first.astype(BF16)
        rest = jnp.zeros((16, TILE), F32)
        for s in range(4):
            shift = (32 * s - o) % TILE
            moved = after[16 * s : 16 * (s + 1), :]
            if shift:
                moved = pltpu.roll(moved, shift, 1)
            rest = jnp.where(short // 32 == s, moved, rest)
        parts[to, WIDTH:PART_ROWS, :] = rest.astype(BF16)


def parts_kernel(depth, parts, gx_out, own, recv, load_sem, ssem, rsem):
    dp = lax.axis_index("dp")
    me_z = lax.axis_index("blk")
    load = pltpu.make_async_copy(parts.at[me_z], own, load_sem)
    load.start()

    def other(d):
        return (me_z + d) % depth

    barrier = pltpu.get_barrier_semaphore()
    for d in range(1, depth):
        pl.semaphore_signal(barrier, inc=1, device_id=(dp, other(d)), device_id_type=MESH)
    pl.semaphore_wait(barrier, depth - 1)

    def z_copy(to, slot):
        return pltpu.make_async_remote_copy(
            src_ref=parts.at[to],
            dst_ref=recv.at[slot],
            send_sem=ssem.at[to],
            recv_sem=rsem.at[slot],
            device_id=(dp, to),
            device_id_type=MESH,
        )

    order = sorted(range(1, depth), key=lambda d: -min(d, depth - d))
    for d in order:
        z_copy(other(d), me_z).start()
    load.wait()
    total = own[...].astype(F32)
    for d in reversed(order):
        source = other(d)
        z_copy(source, source).wait_recv()
        total = total + recv[source].astype(F32)
    gx_out[:, 0:TILE] = total[0:WIDTH, :].astype(BF16)
    rest = total[WIDTH:PART_ROWS, :]
    for s in range(4):
        moved = pltpu.roll(rest, TILE - 32 * s, 1) if s else rest
        gx_out[16 * s : 16 * (s + 1), TILE : TILE + 32] = moved[:, 0:32].astype(BF16)
    for d in range(1, depth):
        z_copy(other(d), me_z).wait_send()


def in_hbm(*arrays):
    return [pltpu.with_memory_space_constraint(array, pltpu.HBM) for array in arrays]


def shards(
    side,
    depth,
    inputs,
    grad_out,
    up_weight,
    gate_weight,
    down_weight,
    saved_gate,
    saved_up,
    block_ids,
    counts,
):
    tokens = TILES * TILE
    units = OWN * BLOCK
    chunk, subs = sizes(side)
    piece = max(piece for _, _, piece in subs)
    stride = stride_of(side)
    dma = pltpu.SemaphoreType.DMA
    anywhere = pl.BlockSpec(memory_space=pl.ANY)
    smem = pl.BlockSpec(memory_space=pltpu.SMEM)
    vmem = pl.BlockSpec(memory_space=pltpu.VMEM)
    go = grad_out.T
    shape = jax.ShapeDtypeStruct
    picked, places = pl.pallas_call(
        pick_kernel,
        out_shape=[shape((TILES, WIDTH, PER * BLOCK), BF16), shape((2 * PAIRS,), jnp.int32)],
        in_specs=[smem, smem, anywhere],
        out_specs=[vmem, smem],
        scratch_shapes=[pltpu.VMEM((WIDTH, units), BF16), dma],
        compiler_params=pltpu.CompilerParams(vmem_limit_bytes=VMEM_LIMIT),
    )(*in_hbm(block_ids, counts, down_weight.T))
    gh, inp, up, gate, sg, su = pl.pallas_call(
        functools.partial(sum_kernel, side),
        out_shape=[
            shape((2, side * stride, BLOCK), BF16),
            shape((WIDTH, tokens), BF16),
            shape((WIDTH, units), BF16),
            shape((WIDTH, units), BF16),
            shape((PAIRS, TILE, BLOCK), BF16),
            shape((PAIRS, TILE, BLOCK), BF16),
        ],
        in_specs=[vmem] * 2 + [anywhere] * 5,
        out_specs=[vmem] * 6,
        scratch_shapes=[
            pltpu.VMEM((HALF, BLOCK), F32),
            pltpu.VMEM((HALF, BLOCK), BF16),
            pltpu.VMEM((HALF, BLOCK), BF16),
            pltpu.VMEM((HALF, BLOCK), BF16),
            pltpu.VMEM((side, chunk, BLOCK), BF16),
            pltpu.VMEM((stride, BLOCK), BF16),
            pltpu.VMEM((SUBS, side, piece, BLOCK), BF16),
            dma((5,)),
            dma((HALF_TILES,)),
            dma((HALF_TILES,)),
        ]
        + [dma((SUBS, side))] * 10,
        compiler_params=pltpu.CompilerParams(
            collective_id=0, has_side_effects=True, vmem_limit_bytes=VMEM_LIMIT
        ),
    )(go, picked, *in_hbm(inputs.T, up_weight, gate_weight, saved_gate[0], saved_up[0]))
    grad_up, grad_gate, grad_down, parts = pl.pallas_call(
        functools.partial(grads_kernel, side, depth),
        out_shape=[shape((WIDTH, units), BF16)] * 3
        + [shape((depth, PART_ROWS, TILE), BF16)],
        in_specs=[smem] + [vmem] * 7,
        out_specs=[vmem] * 4,
        scratch_shapes=[
            pltpu.VMEM((3, OWN, WIDTH, BLOCK), F32),
            pltpu.VMEM((TILES, WIDTH, TILE), F32),
        ],
        compiler_params=pltpu.CompilerParams(vmem_limit_bytes=VMEM_LIMIT),
    )(places, gh, go, inp, up, gate, sg, su)
    grad_x = pl.pallas_call(
        functools.partial(parts_kernel, depth),
        out_shape=shape((WIDTH, tokens // depth), BF16),
        in_specs=[anywhere],
        out_specs=vmem,
        scratch_shapes=[
            pltpu.VMEM((PART_ROWS, TILE), BF16),
            pltpu.VMEM((depth, PART_ROWS, TILE), BF16),
            dma,
            dma((depth,)),
            dma((depth,)),
        ],
        compiler_params=pltpu.CompilerParams(
            collective_id=1, has_side_effects=True, vmem_limit_bytes=VMEM_LIMIT
        ),
    )(parts)
    return (grad_x.T, grad_up, grad_gate, grad_down.T)


def solution(mesh):
    side = 1
    while 2 * side * side < mesh.shape["dp"]:
        side += 1
    in_specs = (
        P(None, "dp"),
        P(None, "dp"),
        P("dp", "blk"),
        P("dp", "blk"),
        P("blk", "dp"),
        P("blk", None, None, None),
        P("blk", None, None, None),
        P(),
        P(),
    )
    out_specs = (P("blk", "dp"), P("dp", "blk"), P("dp", "blk"), P("blk", "dp"))
    return jax.shard_map(
        functools.partial(shards, side, mesh.shape["blk"]),
        mesh=mesh,
        in_specs=in_specs,
        out_specs=out_specs,
        check_vma=False,
    )
```

```python
import functools

import jax
import jax.numpy as jnp
from jax import lax
from jax.experimental import pallas as pl
from jax.experimental.pallas import tpu as pltpu
from jax.sharding import PartitionSpec as P

MESH = pl.DeviceIdType.MESH
BF16 = jnp.bfloat16
F32 = jnp.float32

WIDTH = 64
TILES = 10
TILE = 128
BLOCK = 128
KMAX = 24
PER = 3
PAIRS = TILES * PER
OWN = 28
HALF_PAIRS = PAIRS // 2
HALF_TILES = TILES // 2
HALF = HALF_PAIRS * TILE
PART_ROWS = WIDTH + 16
VMEM_LIMIT = 24 * 1024 * 1024


EARLY = 1
SUBS = 2


def sizes(side):
    chunk = HALF // side
    subs = []
    offset = 0
    for n in range(SUBS):
        number = min(-(-chunk // (SUBS * 16 * side)) * 16 * side, chunk - offset)
        piece = -(-number // side // 16) * 16
        subs.append((offset, number, piece))
        offset += number
    return chunk, subs


def stride_of(side):
    return sum(piece for _, _, piece in sizes(side)[1]) * side


def rows_of(ref, half, place, chunk, stride):
    first = place * TILE
    parts = []
    left = TILE
    while left:
        number, offset = divmod(first, chunk)
        take = min(left, chunk - offset)
        start = number * stride + offset
        parts.append(ref[half, start : start + take, :])
        first += take
        left -= take
    return parts[0] if len(parts) == 1 else jnp.concatenate(parts, axis=0)


def sum_kernel(
    side,
    ids,
    counts,
    go_hbm,
    down_hbm,
    inp_hbm,
    up_hbm,
    gate_hbm,
    sg_hbm,
    su_hbm,
    places,
    gh,
    go,
    inp,
    up,
    gate,
    sg,
    su,
    down,
    picked,
    own,
    half_send,
    half_recv,
    a_send,
    a_recv,
    b_send,
    b_recv,
    load_sem,
    h_ssem,
    h_rsem,
    a_ssem,
    a_rsem,
    b_ssem,
    b_rsem,
    c_ssem,
    c_rsem,
    d_ssem,
    d_rsem,
    f_ssem,
    f_rsem,
):
    chunk, subs = sizes(side)
    stride = stride_of(side)
    dp = lax.axis_index("dp")
    me_z = lax.axis_index("blk")
    core = dp % 2
    me_y = (dp // 2) % side
    me_x = dp // (2 * side)
    partner = dp + 1 - 2 * core
    me_a = me_x + core * (me_y - me_x)
    me_b = me_y + core * (me_x - me_y)
    step_a = (1 - core) * 2 * side + core * 2
    step_b = (1 - core) * 2 + core * 2 * side

    def along_a(i):
        return dp + (i - me_a) * step_a

    def along_b(i):
        return dp + (i - me_b) * step_b

    def other(me, d):
        return (me + d) % side

    barrier = pltpu.get_barrier_semaphore()
    pl.semaphore_signal(barrier, inc=1, device_id=(partner, me_z), device_id_type=MESH)
    for d in range(1, side):
        pl.semaphore_signal(
            barrier, inc=1, device_id=(along_a(other(me_a, d)), me_z), device_id_type=MESH
        )
        pl.semaphore_signal(
            barrier, inc=1, device_id=(along_b(other(me_b, d)), me_z), device_id_type=MESH
        )

    loads = [
        pltpu.make_async_copy(source, target, load_sem.at[i])
        for i, (source, target) in enumerate(
            (
                (down_hbm, down),
                (go_hbm, go),
                (inp_hbm, inp),
                (up_hbm, up),
                (gate_hbm, gate),
                (sg_hbm, sg),
                (su_hbm, su),
            )
        )
    ]
    for load in loads:
        load.start()

    low = me_z * OWN

    first = jnp.int32(0)
    for t in range(TILES):
        live = counts[t]
        packed = jnp.int32(0)
        shift = jnp.int32(0)
        for k in range(KMAX):
            block = ids[t, k] - low
            owned = (block >= 0) & (block < OWN) & (live > k)
            packed = packed + jnp.where(owned, lax.shift_left(block + 1, shift), 0)
            shift = shift + jnp.where(owned, 5, 0)
        number = jnp.int32(0)
        for j in range(PER):
            place = lax.shift_right_logical(packed, jnp.int32(5 * j)) & 31
            places[t * PER + j] = place
            places[PAIRS + t * PER + j] = jnp.minimum(first + j, PAIRS - 1)
            number = number + jnp.where(place > 0, 1, 0)
        first = first + number

    loads[0].wait()
    for t in range(TILES):
        wanted = [places[t * PER + j] for j in range(PER)]
        found = [down[:, 0:BLOCK]] * PER
        for b in range(1, OWN):
            block = down[:, b * BLOCK : (b + 1) * BLOCK]
            found = [jnp.where(w == b + 1, block, f) for w, f in zip(wanted, found)]
        for j in range(PER):
            picked[t, :, j * BLOCK : (j + 1) * BLOCK] = found[j]
    loads[1].wait()

    def hidden_terms(t):
        tokens = go[:, pl.ds(pl.multiple_of(t * TILE, TILE), TILE)]
        return lax.dot_general(
            tokens, picked[t], (((0,), (0,)), ((), ())), preferred_element_type=F32
        )

    def h_copy(i):
        rows = pl.ds(i * PER * TILE, PER * TILE)
        return pltpu.make_async_remote_copy(
            src_ref=half_send.at[rows],
            dst_ref=half_recv.at[rows],
            send_sem=h_ssem.at[i],
            recv_sem=h_rsem.at[i],
            device_id=(partner, me_z),
            device_id_type=MESH,
        )

    for i in range(HALF_TILES):
        others = hidden_terms((1 - core) * HALF_TILES + i)
        for j in range(PER):
            start = (i * PER + j) * TILE
            half_send[start : start + TILE, :] = others[:, j * BLOCK : (j + 1) * BLOCK].astype(BF16)
    for i in range(HALF_TILES):
        mine = hidden_terms(core * HALF_TILES + i)
        for j in range(PER):
            start = (i * PER + j) * TILE
            own[start : start + TILE, :] = mine[:, j * BLOCK : (j + 1) * BLOCK]
        if i == EARLY:
            pl.semaphore_wait(barrier, 1 + 2 * (side - 1))
            for k in range(HALF_TILES):
                h_copy(k).start()
    for i in range(HALF_TILES):
        h_copy(i).wait_recv()
        rows = slice(i * PER * TILE, (i + 1) * PER * TILE)
        a_send[rows, :] = (own[rows, :] + half_recv[rows, :].astype(F32)).astype(BF16)

    def a_copy(to, slot, n):
        offset, number, _ = subs[n]
        rows = pl.ds(pl.multiple_of(to * chunk + offset, 16), number)
        return pltpu.make_async_remote_copy(
            src_ref=a_send.at[rows],
            dst_ref=a_recv.at[slot, offset : offset + number],
            send_sem=a_ssem.at[n, to],
            recv_sem=a_rsem.at[n, slot],
            device_id=(along_a(to), me_z),
            device_id_type=MESH,
        )

    def b_copy(to, slot, n):
        offset, _, piece = subs[n]
        rows = pl.ds(pl.multiple_of(offset + to * piece, 16), piece)
        return pltpu.make_async_remote_copy(
            src_ref=b_send.at[rows],
            dst_ref=b_recv.at[n, slot, 0:piece],
            send_sem=b_ssem.at[n, to],
            recv_sem=b_rsem.at[n, slot],
            device_id=(along_b(to), me_z),
            device_id_type=MESH,
        )

    def c_copy(to, slot, n):
        offset, _, piece = subs[n]
        rows = pl.ds(pl.multiple_of(me_a * stride + offset + slot * piece, 16), piece)
        return pltpu.make_async_remote_copy(
            src_ref=gh.at[core, rows],
            dst_ref=gh.at[core, rows],
            send_sem=c_ssem.at[n, to],
            recv_sem=c_rsem.at[n, slot],
            device_id=(along_b(to), me_z),
            device_id_type=MESH,
        )

    def d_copy(to, slot, n):
        offset, number, _ = subs[n]
        rows = pl.ds(pl.multiple_of(slot * stride + offset, 16), number)
        return pltpu.make_async_remote_copy(
            src_ref=gh.at[core, rows],
            dst_ref=gh.at[core, rows],
            send_sem=d_ssem.at[n, to],
            recv_sem=d_rsem.at[n, slot],
            device_id=(along_a(to), me_z),
            device_id_type=MESH,
        )

    def f_copy(slot, half, n):
        offset, number, _ = subs[n]
        rows = pl.ds(pl.multiple_of(slot * stride + offset, 16), number)
        return pltpu.make_async_remote_copy(
            src_ref=gh.at[half, rows],
            dst_ref=gh.at[half, rows],
            send_sem=f_ssem.at[n, slot],
            recv_sem=f_rsem.at[n, slot],
            device_id=(partner, me_z),
            device_id_type=MESH,
        )

    order = sorted(range(1, side), key=lambda d: -min(d, side - d))
    steps = range(len(subs))
    for n in steps:
        for d in order:
            a_copy(other(me_a, d), me_a, n).start()
    for n in steps:
        offset, number, piece = subs[n]
        rows = pl.ds(pl.multiple_of(me_a * chunk + offset, 16), number)
        total = a_send[rows, :].astype(F32)
        for d in reversed(order):
            source = other(me_a, d)
            a_copy(source, source, n).wait_recv()
            total = total + a_recv[source, offset : offset + number, :].astype(F32)
        b_send[offset : offset + number, :] = total.astype(BF16)
        end = offset + piece * side
        if end > offset + number:
            b_send[offset + number : end, :] = jnp.zeros((end - offset - number, BLOCK), BF16)
        for d in order:
            b_copy(other(me_b, d), me_b, n).start()
    for n in steps:
        offset, _, piece = subs[n]
        total = b_send[pl.ds(pl.multiple_of(offset + me_b * piece, 16), piece), :].astype(F32)
        for d in reversed(order):
            source = other(me_b, d)
            b_copy(source, source, n).wait_recv()
            total = total + b_recv[n, source, 0:piece, :].astype(F32)
        rows = pl.ds(pl.multiple_of(me_a * stride + offset + me_b * piece, 16), piece)
        gh[core, rows, :] = total.astype(BF16)
        for d in order:
            c_copy(other(me_b, d), me_b, n).start()
    for n in steps:
        for d in reversed(order):
            source = other(me_b, d)
            c_copy(source, source, n).wait_recv()
        for d in order:
            d_copy(other(me_a, d), me_a, n).start()
        f_copy(me_a, core, n).start()
    for n in steps:
        for d in reversed(order):
            source = other(me_a, d)
            d_copy(source, source, n).wait_recv()
            f_copy(source, core, n).start()
    for n in steps:
        for d in range(side):
            f_copy(d, 1 - core, n).wait_recv()

    for load in loads[2:]:
        load.wait()
    for i in range(HALF_TILES):
        h_copy(i).wait_send()
    for n in steps:
        for d in range(1, side):
            a_copy(other(me_a, d), me_a, n).wait_send()
            b_copy(other(me_b, d), me_b, n).wait_send()
            c_copy(other(me_b, d), me_b, n).wait_send()
            d_copy(other(me_a, d), me_a, n).wait_send()
        for d in range(side):
            f_copy(d, core, n).wait_send()


def grads_kernel(
    side,
    depth,
    places,
    gh,
    go,
    inp,
    up,
    gate,
    sg,
    su,
    up_out,
    gate_out,
    down_out,
    parts,
    totals,
    gx,
):
    chunk, _ = sizes(side)
    stride = stride_of(side)
    totals[...] = jnp.zeros_like(totals)
    for t in range(TILES):
        half, i = divmod(t, HALF_TILES)
        weights = []
        values = []
        tokens = slice(t * TILE, (t + 1) * TILE)
        for j in range(PER):
            number = t * PER + j
            place = places[number]
            slot = places[PAIRS + number]
            live = jnp.where(place > 0, jnp.float32(1), jnp.float32(0))
            block = jnp.maximum(place - 1, 0)
            gate_value = sg[slot].astype(F32)
            up_value = su[slot].astype(F32)
            positive = jnp.maximum(gate_value, 0.0) * live
            value = rows_of(gh, half, i * PER + j, chunk, stride).astype(F32)
            hidden = (positive * up_value).astype(BF16)
            grad_up = (value * positive).astype(BF16)
            grad_gate = (value * (jnp.where(gate_value > 0, up_value, 0.0) * live)).astype(BF16)
            columns = pl.ds(pl.multiple_of(block * BLOCK, BLOCK), BLOCK)
            weights += [up[:, columns], gate[:, columns]]
            values += [grad_up, grad_gate]
            pair = jnp.dot(
                inp[:, tokens],
                jnp.concatenate([grad_up, grad_gate], axis=1),
                preferred_element_type=F32,
            )
            totals[0, block] += pair[:, 0:BLOCK]
            totals[1, block] += pair[:, BLOCK : 2 * BLOCK]
            totals[2, block] += jnp.dot(go[:, tokens], hidden, preferred_element_type=F32)
        gx[t] = lax.dot_general(
            jnp.concatenate(weights, axis=1),
            jnp.concatenate(values, axis=1),
            (((1,), (1,)), ((), ())),
            preferred_element_type=F32,
        )
    for i, out in enumerate((up_out, gate_out, down_out)):
        for b in range(OWN):
            out[:, b * BLOCK : (b + 1) * BLOCK] = totals[i, b].astype(BF16)

    lanes = lax.broadcasted_iota(jnp.int32, (WIDTH, TILE), 1)
    short = lax.broadcasted_iota(jnp.int32, (16, TILE), 1)
    for to in range(depth):
        q, o = divmod(to * TILES * TILE // depth, TILE)
        after = gx[q + 1]
        if o:
            first = jnp.where(
                lanes < TILE - o,
                pltpu.roll(gx[q], TILE - o, 1),
                pltpu.roll(after, TILE - o, 1),
            )
        else:
            first = gx[q]
        parts[to, 0:WIDTH, :] = first.astype(BF16)
        rest = jnp.zeros((16, TILE), F32)
        for s in range(4):
            shift = (32 * s - o) % TILE
            moved = after[16 * s : 16 * (s + 1), :]
            if shift:
                moved = pltpu.roll(moved, shift, 1)
            rest = jnp.where(short // 32 == s, moved, rest)
        parts[to, WIDTH:PART_ROWS, :] = rest.astype(BF16)


def parts_kernel(depth, parts, gx_out, own, recv, load_sem, ssem, rsem):
    dp = lax.axis_index("dp")
    me_z = lax.axis_index("blk")
    load = pltpu.make_async_copy(parts.at[me_z], own, load_sem)
    load.start()

    def other(d):
        return (me_z + d) % depth

    barrier = pltpu.get_barrier_semaphore()
    for d in range(1, depth):
        pl.semaphore_signal(barrier, inc=1, device_id=(dp, other(d)), device_id_type=MESH)
    pl.semaphore_wait(barrier, depth - 1)

    def z_copy(to, slot):
        return pltpu.make_async_remote_copy(
            src_ref=parts.at[to],
            dst_ref=recv.at[slot],
            send_sem=ssem.at[to],
            recv_sem=rsem.at[slot],
            device_id=(dp, to),
            device_id_type=MESH,
        )

    order = sorted(range(1, depth), key=lambda d: -min(d, depth - d))
    for d in order:
        z_copy(other(d), me_z).start()
    load.wait()
    total = own[...].astype(F32)
    for d in reversed(order):
        source = other(d)
        z_copy(source, source).wait_recv()
        total = total + recv[source].astype(F32)
    gx_out[:, 0:TILE] = total[0:WIDTH, :].astype(BF16)
    rest = total[WIDTH:PART_ROWS, :]
    for s in range(4):
        moved = pltpu.roll(rest, TILE - 32 * s, 1) if s else rest
        gx_out[16 * s : 16 * (s + 1), TILE : TILE + 32] = moved[:, 0:32].astype(BF16)
    for d in range(1, depth):
        z_copy(other(d), me_z).wait_send()


def in_hbm(*arrays):
    return [pltpu.with_memory_space_constraint(array, pltpu.HBM) for array in arrays]


def shards(
    side,
    depth,
    inputs,
    grad_out,
    up_weight,
    gate_weight,
    down_weight,
    saved_gate,
    saved_up,
    block_ids,
    counts,
):
    tokens = TILES * TILE
    units = OWN * BLOCK
    chunk, subs = sizes(side)
    piece = max(piece for _, _, piece in subs)
    stride = stride_of(side)
    dma = pltpu.SemaphoreType.DMA
    anywhere = pl.BlockSpec(memory_space=pl.ANY)
    smem = pl.BlockSpec(memory_space=pltpu.SMEM)
    vmem = pl.BlockSpec(memory_space=pltpu.VMEM)
    shape = jax.ShapeDtypeStruct
    places, gh, go, inp, up, gate, sg, su = pl.pallas_call(
        functools.partial(sum_kernel, side),
        out_shape=[
            shape((2 * PAIRS,), jnp.int32),
            shape((2, side * stride, BLOCK), BF16),
            shape((WIDTH, tokens), BF16),
            shape((WIDTH, tokens), BF16),
            shape((WIDTH, units), BF16),
            shape((WIDTH, units), BF16),
            shape((PAIRS, TILE, BLOCK), BF16),
            shape((PAIRS, TILE, BLOCK), BF16),
        ],
        in_specs=[smem] * 2 + [anywhere] * 7,
        out_specs=[smem] + [vmem] * 7,
        scratch_shapes=[
            pltpu.VMEM((WIDTH, units), BF16),
            pltpu.VMEM((TILES, WIDTH, PER * BLOCK), BF16),
            pltpu.VMEM((HALF, BLOCK), F32),
            pltpu.VMEM((HALF, BLOCK), BF16),
            pltpu.VMEM((HALF, BLOCK), BF16),
            pltpu.VMEM((HALF, BLOCK), BF16),
            pltpu.VMEM((side, chunk, BLOCK), BF16),
            pltpu.VMEM((stride, BLOCK), BF16),
            pltpu.VMEM((SUBS, side, piece, BLOCK), BF16),
            dma((7,)),
            dma((HALF_TILES,)),
            dma((HALF_TILES,)),
        ]
        + [dma((SUBS, side))] * 10,
        compiler_params=pltpu.CompilerParams(
            collective_id=0, has_side_effects=True, vmem_limit_bytes=VMEM_LIMIT
        ),
    )(
        *in_hbm(
            block_ids,
            counts,
            grad_out.T,
            down_weight.T,
            inputs.T,
            up_weight,
            gate_weight,
            saved_gate[0],
            saved_up[0],
        )
    )
    grad_up, grad_gate, grad_down, parts = pl.pallas_call(
        functools.partial(grads_kernel, side, depth),
        out_shape=[shape((WIDTH, units), BF16)] * 3
        + [shape((depth, PART_ROWS, TILE), BF16)],
        in_specs=[smem] + [vmem] * 7,
        out_specs=[vmem] * 4,
        scratch_shapes=[
            pltpu.VMEM((3, OWN, WIDTH, BLOCK), F32),
            pltpu.VMEM((TILES, WIDTH, TILE), F32),
        ],
        compiler_params=pltpu.CompilerParams(vmem_limit_bytes=VMEM_LIMIT),
    )(places, gh, go, inp, up, gate, sg, su)
    grad_x = pl.pallas_call(
        functools.partial(parts_kernel, depth),
        out_shape=shape((WIDTH, tokens // depth), BF16),
        in_specs=[anywhere],
        out_specs=vmem,
        scratch_shapes=[
            pltpu.VMEM((PART_ROWS, TILE), BF16),
            pltpu.VMEM((depth, PART_ROWS, TILE), BF16),
            dma,
            dma((depth,)),
            dma((depth,)),
        ],
        compiler_params=pltpu.CompilerParams(
            collective_id=1, has_side_effects=True, vmem_limit_bytes=VMEM_LIMIT
        ),
    )(parts)
    return (grad_x.T, grad_up, grad_gate, grad_down.T)


def solution(mesh):
    side = 1
    while 2 * side * side < mesh.shape["dp"]:
        side += 1
    in_specs = (
        P(None, "dp"),
        P(None, "dp"),
        P("dp", "blk"),
        P("dp", "blk"),
        P("blk", "dp"),
        P("blk", None, None, None),
        P("blk", None, None, None),
        P(),
        P(),
    )
    out_specs = (P("blk", "dp"), P("dp", "blk"), P("dp", "blk"), P("blk", "dp"))
    return jax.shard_map(
        functools.partial(shards, side, mesh.shape["blk"]),
        mesh=mesh,
        in_specs=in_specs,
        out_specs=out_specs,
        check_vma=False,
    )
```

```python
import functools

import jax
import jax.numpy as jnp
from jax import lax
from jax.experimental import pallas as pl
from jax.experimental.pallas import tpu as pltpu
from jax.sharding import PartitionSpec as P

MESH = pl.DeviceIdType.MESH
BF16 = jnp.bfloat16
F32 = jnp.float32

WIDTH = 64
TILES = 10
TILE = 128
BLOCK = 128
KMAX = 24
PER = 3
PAIRS = TILES * PER
OWN = 28
HALF_PAIRS = PAIRS // 2
HALF_TILES = TILES // 2
HALF = HALF_PAIRS * TILE
PART_ROWS = WIDTH + 16
VMEM_LIMIT = 24 * 1024 * 1024


EARLY = 1
SUBS = 2


def sizes(side):
    chunk = HALF // side
    subs = []
    offset = 0
    for n in range(SUBS):
        number = min(-(-chunk // (SUBS * 16 * side)) * 16 * side, chunk - offset)
        piece = -(-number // side // 16) * 16
        subs.append((offset, number, piece))
        offset += number
    return chunk, subs


def stride_of(side):
    return sum(piece for _, _, piece in sizes(side)[1]) * side


def rows_of(ref, half, place, chunk, stride):
    first = place * TILE
    parts = []
    left = TILE
    while left:
        number, offset = divmod(first, chunk)
        take = min(left, chunk - offset)
        start = number * stride + offset
        parts.append(ref[half, start : start + take, :])
        first += take
        left -= take
    return parts[0] if len(parts) == 1 else jnp.concatenate(parts, axis=0)


def sum_kernel(
    side,
    depth,
    ids,
    counts,
    go_hbm,
    down_hbm,
    inp_hbm,
    up_hbm,
    gate_hbm,
    sg_hbm,
    su_hbm,
    places,
    gx_out,
    pairs,
    go,
    inp,
    up,
    gate,
    sg,
    su,
    gh,
    weights,
    gx,
    z_send,
    z_recv,
    down,
    picked,
    own,
    half_send,
    half_recv,
    a_send,
    a_recv,
    b_send,
    b_recv,
    load_sem,
    h_ssem,
    h_rsem,
    a_ssem,
    a_rsem,
    b_ssem,
    b_rsem,
    c_ssem,
    c_rsem,
    d_ssem,
    d_rsem,
    f_ssem,
    f_rsem,
    z_ssem,
    z_rsem,
):
    chunk, subs = sizes(side)
    stride = stride_of(side)
    dp = lax.axis_index("dp")
    me_z = lax.axis_index("blk")
    core = dp % 2
    me_y = (dp // 2) % side
    me_x = dp // (2 * side)
    partner = dp + 1 - 2 * core
    me_a = me_x + core * (me_y - me_x)
    me_b = me_y + core * (me_x - me_y)
    step_a = (1 - core) * 2 * side + core * 2
    step_b = (1 - core) * 2 + core * 2 * side

    def along_a(i):
        return dp + (i - me_a) * step_a

    def along_b(i):
        return dp + (i - me_b) * step_b

    def other(me, d):
        return (me + d) % side

    barrier = pltpu.get_barrier_semaphore()
    pl.semaphore_signal(barrier, inc=1, device_id=(partner, me_z), device_id_type=MESH)
    for d in range(1, side):
        pl.semaphore_signal(
            barrier, inc=1, device_id=(along_a(other(me_a, d)), me_z), device_id_type=MESH
        )
        pl.semaphore_signal(
            barrier, inc=1, device_id=(along_b(other(me_b, d)), me_z), device_id_type=MESH
        )

    for d in range(1, depth):
        pl.semaphore_signal(
            barrier, inc=1, device_id=(dp, (me_z + d) % depth), device_id_type=MESH
        )

    loads = [
        pltpu.make_async_copy(source, target, load_sem.at[i])
        for i, (source, target) in enumerate(
            (
                (down_hbm, down),
                (go_hbm, go),
                (inp_hbm, inp),
                (up_hbm, up),
                (gate_hbm, gate),
                (sg_hbm, sg),
                (su_hbm, su),
            )
        )
    ]
    for load in loads:
        load.start()

    low = me_z * OWN

    first = jnp.int32(0)
    for t in range(TILES):
        live = counts[t]
        packed = jnp.int32(0)
        shift = jnp.int32(0)
        for k in range(KMAX):
            block = ids[t, k] - low
            owned = (block >= 0) & (block < OWN) & (live > k)
            packed = packed + jnp.where(owned, lax.shift_left(block + 1, shift), 0)
            shift = shift + jnp.where(owned, 5, 0)
        number = jnp.int32(0)
        for j in range(PER):
            place = lax.shift_right_logical(packed, jnp.int32(5 * j)) & 31
            places[t * PER + j] = place
            places[PAIRS + t * PER + j] = jnp.minimum(first + j, PAIRS - 1)
            number = number + jnp.where(place > 0, 1, 0)
        first = first + number

    loads[0].wait()
    for t in range(TILES):
        wanted = [places[t * PER + j] for j in range(PER)]
        found = [down[:, 0:BLOCK]] * PER
        for b in range(1, OWN):
            block = down[:, b * BLOCK : (b + 1) * BLOCK]
            found = [jnp.where(w == b + 1, block, f) for w, f in zip(wanted, found)]
        for j in range(PER):
            picked[t, :, j * BLOCK : (j + 1) * BLOCK] = found[j]
    loads[1].wait()

    def hidden_terms(t):
        tokens = go[:, pl.ds(pl.multiple_of(t * TILE, TILE), TILE)]
        return lax.dot_general(
            tokens, picked[t], (((0,), (0,)), ((), ())), preferred_element_type=F32
        )

    def h_copy(i):
        rows = pl.ds(i * PER * TILE, PER * TILE)
        return pltpu.make_async_remote_copy(
            src_ref=half_send.at[rows],
            dst_ref=half_recv.at[rows],
            send_sem=h_ssem.at[i],
            recv_sem=h_rsem.at[i],
            device_id=(partner, me_z),
            device_id_type=MESH,
        )

    for i in range(HALF_TILES):
        others = hidden_terms((1 - core) * HALF_TILES + i)
        for j in range(PER):
            start = (i * PER + j) * TILE
            half_send[start : start + TILE, :] = others[:, j * BLOCK : (j + 1) * BLOCK].astype(BF16)
    for i in range(HALF_TILES):
        mine = hidden_terms(core * HALF_TILES + i)
        for j in range(PER):
            start = (i * PER + j) * TILE
            own[start : start + TILE, :] = mine[:, j * BLOCK : (j + 1) * BLOCK]
        if i == EARLY:
            pl.semaphore_wait(barrier, 1 + 2 * (side - 1) + depth - 1)
            for k in range(HALF_TILES):
                h_copy(k).start()
    for i in range(HALF_TILES):
        h_copy(i).wait_recv()
        rows = slice(i * PER * TILE, (i + 1) * PER * TILE)
        a_send[rows, :] = (own[rows, :] + half_recv[rows, :].astype(F32)).astype(BF16)

    def a_copy(to, slot, n):
        offset, number, _ = subs[n]
        rows = pl.ds(pl.multiple_of(to * chunk + offset, 16), number)
        return pltpu.make_async_remote_copy(
            src_ref=a_send.at[rows],
            dst_ref=a_recv.at[slot, offset : offset + number],
            send_sem=a_ssem.at[n, to],
            recv_sem=a_rsem.at[n, slot],
            device_id=(along_a(to), me_z),
            device_id_type=MESH,
        )

    def b_copy(to, slot, n):
        offset, _, piece = subs[n]
        rows = pl.ds(pl.multiple_of(offset + to * piece, 16), piece)
        return pltpu.make_async_remote_copy(
            src_ref=b_send.at[rows],
            dst_ref=b_recv.at[n, slot, 0:piece],
            send_sem=b_ssem.at[n, to],
            recv_sem=b_rsem.at[n, slot],
            device_id=(along_b(to), me_z),
            device_id_type=MESH,
        )

    def c_copy(to, slot, n):
        offset, _, piece = subs[n]
        rows = pl.ds(pl.multiple_of(me_a * stride + offset + slot * piece, 16), piece)
        return pltpu.make_async_remote_copy(
            src_ref=gh.at[core, rows],
            dst_ref=gh.at[core, rows],
            send_sem=c_ssem.at[n, to],
            recv_sem=c_rsem.at[n, slot],
            device_id=(along_b(to), me_z),
            device_id_type=MESH,
        )

    def d_copy(to, slot, n):
        offset, number, _ = subs[n]
        rows = pl.ds(pl.multiple_of(slot * stride + offset, 16), number)
        return pltpu.make_async_remote_copy(
            src_ref=gh.at[core, rows],
            dst_ref=gh.at[core, rows],
            send_sem=d_ssem.at[n, to],
            recv_sem=d_rsem.at[n, slot],
            device_id=(along_a(to), me_z),
            device_id_type=MESH,
        )

    def f_copy(slot, half, n):
        offset, number, _ = subs[n]
        rows = pl.ds(pl.multiple_of(slot * stride + offset, 16), number)
        return pltpu.make_async_remote_copy(
            src_ref=gh.at[half, rows],
            dst_ref=gh.at[half, rows],
            send_sem=f_ssem.at[n, slot],
            recv_sem=f_rsem.at[n, slot],
            device_id=(partner, me_z),
            device_id_type=MESH,
        )

    order = sorted(range(1, side), key=lambda d: -min(d, side - d))
    steps = range(len(subs))
    for n in steps:
        for d in order:
            a_copy(other(me_a, d), me_a, n).start()

    loads[5].wait()
    loads[6].wait()
    for number in range(PAIRS):
        t, j = divmod(number, PER)
        slot = places[PAIRS + number]
        live = jnp.where(places[number] > 0, jnp.float32(1), jnp.float32(0))
        gate_value = sg[j]
        up_value = su[j]
        for c in range(j + 1, min(t * PER + j, PAIRS - 1) + 1):
            gate_value = jnp.where(slot == c, sg[c], gate_value)
            up_value = jnp.where(slot == c, su[c], up_value)
        gate_value = gate_value.astype(F32)
        up_value = up_value.astype(F32)
        positive = jnp.maximum(gate_value, 0.0) * live
        pairs[number, :, 0:BLOCK] = positive.astype(BF16)
        pairs[number, :, BLOCK : 2 * BLOCK] = (
            jnp.where(gate_value > 0, up_value, 0.0) * live
        ).astype(BF16)
        pairs[number, :, 2 * BLOCK : 3 * BLOCK] = (positive * up_value).astype(BF16)

    for n in steps:
        offset, number, piece = subs[n]
        rows = pl.ds(pl.multiple_of(me_a * chunk + offset, 16), number)
        total = a_send[rows, :].astype(F32)
        for d in reversed(order):
            source = other(me_a, d)
            a_copy(source, source, n).wait_recv()
            total = total + a_recv[source, offset : offset + number, :].astype(F32)
        b_send[offset : offset + number, :] = total.astype(BF16)
        end = offset + piece * side
        if end > offset + number:
            b_send[offset + number : end, :] = jnp.zeros((end - offset - number, BLOCK), BF16)
        for d in order:
            b_copy(other(me_b, d), me_b, n).start()
    for n in steps:
        offset, _, piece = subs[n]
        total = b_send[pl.ds(pl.multiple_of(offset + me_b * piece, 16), piece), :].astype(F32)
        for d in reversed(order):
            source = other(me_b, d)
            b_copy(source, source, n).wait_recv()
            total = total + b_recv[n, source, 0:piece, :].astype(F32)
        rows = pl.ds(pl.multiple_of(me_a * stride + offset + me_b * piece, 16), piece)
        gh[core, rows, :] = total.astype(BF16)
        for d in order:
            c_copy(other(me_b, d), me_b, n).start()
    for n in steps:
        for d in reversed(order):
            source = other(me_b, d)
            c_copy(source, source, n).wait_recv()
        for d in order:
            d_copy(other(me_a, d), me_a, n).start()
        f_copy(me_a, core, n).start()

    loads[3].wait()
    loads[4].wait()
    for t in range(TILES):
        wanted = [places[t * PER + j] for j in range(PER)]
        for k, source in enumerate((up, gate)):
            found = [source[:, 0:BLOCK]] * PER
            for b in range(1, OWN):
                block = source[:, b * BLOCK : (b + 1) * BLOCK]
                found = [jnp.where(w == b + 1, block, f) for w, f in zip(wanted, found)]
            for j in range(PER):
                weights[t, :, (2 * j + k) * BLOCK : (2 * j + k + 1) * BLOCK] = found[j]

    for n in steps:
        for d in reversed(order):
            source = other(me_a, d)
            d_copy(source, source, n).wait_recv()
            f_copy(source, core, n).start()
    for n in steps:
        for d in range(side):
            f_copy(d, 1 - core, n).wait_recv()

    for t in range(TILES):
        half, i = divmod(t, HALF_TILES)
        values = []
        for j in range(PER):
            number = t * PER + j
            value = rows_of(gh, half, i * PER + j, chunk, stride).astype(F32)
            for k in range(2):
                lanes = slice(k * BLOCK, (k + 1) * BLOCK)
                grad = (value * pairs[number, :, lanes].astype(F32)).astype(BF16)
                pairs[number, :, lanes] = grad
                values.append(grad)
        gx[t] = lax.dot_general(
            weights[t],
            jnp.concatenate(values, axis=1),
            (((1,), (1,)), ((), ())),
            preferred_element_type=F32,
        )

    lanes = lax.broadcasted_iota(jnp.int32, (WIDTH, TILE), 1)
    short = lax.broadcasted_iota(jnp.int32, (16, TILE), 1)
    for to in range(depth):
        q, o = divmod(to * TILES * TILE // depth, TILE)
        after = gx[q + 1]
        if o:
            first = jnp.where(
                lanes < TILE - o,
                pltpu.roll(gx[q], TILE - o, 1),
                pltpu.roll(after, TILE - o, 1),
            )
        else:
            first = gx[q]
        z_send[to, 0:WIDTH, :] = first.astype(BF16)
        rest = jnp.zeros((16, TILE), F32)
        for s in range(4):
            shift = (32 * s - o) % TILE
            moved = after[16 * s : 16 * (s + 1), :]
            if shift:
                moved = pltpu.roll(moved, shift, 1)
            rest = jnp.where(short // 32 == s, moved, rest)
        z_send[to, WIDTH:PART_ROWS, :] = rest.astype(BF16)

    def z_copy(to, slot):
        return pltpu.make_async_remote_copy(
            src_ref=z_send.at[to],
            dst_ref=z_recv.at[slot],
            send_sem=z_ssem.at[to],
            recv_sem=z_rsem.at[slot],
            device_id=(dp, to),
            device_id_type=MESH,
        )

    z_order = sorted(range(1, depth), key=lambda d: -min(d, depth - d))
    for d in z_order:
        z_copy((me_z + d) % depth, me_z).start()
    total = z_send[me_z].astype(F32)
    for d in reversed(z_order):
        source = (me_z + d) % depth
        z_copy(source, source).wait_recv()
        total = total + z_recv[source].astype(F32)
    gx_out[:, 0:TILE] = total[0:WIDTH, :].astype(BF16)
    rest = total[WIDTH:PART_ROWS, :]
    for s in range(4):
        moved = pltpu.roll(rest, TILE - 32 * s, 1) if s else rest
        gx_out[16 * s : 16 * (s + 1), TILE : TILE + 32] = moved[:, 0:32].astype(BF16)
    for d in range(1, depth):
        z_copy((me_z + d) % depth, me_z).wait_send()

    loads[2].wait()
    for i in range(HALF_TILES):
        h_copy(i).wait_send()
    for n in steps:
        for d in range(1, side):
            a_copy(other(me_a, d), me_a, n).wait_send()
            b_copy(other(me_b, d), me_b, n).wait_send()
            c_copy(other(me_b, d), me_b, n).wait_send()
            d_copy(other(me_a, d), me_a, n).wait_send()
        for d in range(side):
            f_copy(d, core, n).wait_send()


def grads_kernel(places, pairs, go, inp, up_out, gate_out, down_out, totals):
    totals[...] = jnp.zeros_like(totals)
    for number in range(PAIRS):
        t = number // PER
        tokens = slice(t * TILE, (t + 1) * TILE)
        block = jnp.maximum(places[number] - 1, 0)
        pair = jnp.dot(
            inp[:, tokens], pairs[number, :, 0 : 2 * BLOCK], preferred_element_type=F32
        )
        totals[0, block] += pair[:, 0:BLOCK]
        totals[1, block] += pair[:, BLOCK : 2 * BLOCK]
        totals[2, block] += jnp.dot(
            go[:, tokens], pairs[number, :, 2 * BLOCK : 3 * BLOCK], preferred_element_type=F32
        )
    for i, out in enumerate((up_out, gate_out, down_out)):
        for b in range(OWN):
            out[:, b * BLOCK : (b + 1) * BLOCK] = totals[i, b].astype(BF16)


def in_hbm(*arrays):
    return [pltpu.with_memory_space_constraint(array, pltpu.HBM) for array in arrays]


def shards(
    side,
    depth,
    inputs,
    grad_out,
    up_weight,
    gate_weight,
    down_weight,
    saved_gate,
    saved_up,
    block_ids,
    counts,
):
    tokens = TILES * TILE
    units = OWN * BLOCK
    chunk, subs = sizes(side)
    piece = max(piece for _, _, piece in subs)
    stride = stride_of(side)
    dma = pltpu.SemaphoreType.DMA
    anywhere = pl.BlockSpec(memory_space=pl.ANY)
    smem = pl.BlockSpec(memory_space=pltpu.SMEM)
    vmem = pl.BlockSpec(memory_space=pltpu.VMEM)
    shape = jax.ShapeDtypeStruct
    places, grad_x, pairs, go, inp = pl.pallas_call(
        functools.partial(sum_kernel, side, depth),
        out_shape=[
            shape((2 * PAIRS,), jnp.int32),
            shape((WIDTH, tokens // depth), BF16),
            shape((PAIRS, TILE, 3 * BLOCK), BF16),
            shape((WIDTH, tokens), BF16),
            shape((WIDTH, tokens), BF16),
        ],
        in_specs=[smem] * 2 + [anywhere] * 7,
        out_specs=[smem] + [vmem] * 4,
        scratch_shapes=[
            pltpu.VMEM((WIDTH, units), BF16),
            pltpu.VMEM((WIDTH, units), BF16),
            pltpu.VMEM((PAIRS, TILE, BLOCK), BF16),
            pltpu.VMEM((PAIRS, TILE, BLOCK), BF16),
            pltpu.VMEM((2, side * stride, BLOCK), BF16),
            pltpu.VMEM((TILES, WIDTH, 2 * PER * BLOCK), BF16),
            pltpu.VMEM((TILES, WIDTH, TILE), F32),
            pltpu.VMEM((depth, PART_ROWS, TILE), BF16),
            pltpu.VMEM((depth, PART_ROWS, TILE), BF16),
            pltpu.VMEM((WIDTH, units), BF16),
            pltpu.VMEM((TILES, WIDTH, PER * BLOCK), BF16),
            pltpu.VMEM((HALF, BLOCK), F32),
            pltpu.VMEM((HALF, BLOCK), BF16),
            pltpu.VMEM((HALF, BLOCK), BF16),
            pltpu.VMEM((HALF, BLOCK), BF16),
            pltpu.VMEM((side, chunk, BLOCK), BF16),
            pltpu.VMEM((stride, BLOCK), BF16),
            pltpu.VMEM((SUBS, side, piece, BLOCK), BF16),
            dma((7,)),
            dma((HALF_TILES,)),
            dma((HALF_TILES,)),
        ]
        + [dma((SUBS, side))] * 10
        + [dma((depth,))] * 2,
        compiler_params=pltpu.CompilerParams(
            collective_id=0, has_side_effects=True, vmem_limit_bytes=VMEM_LIMIT
        ),
    )(
        *in_hbm(
            block_ids,
            counts,
            grad_out.T,
            down_weight.T,
            inputs.T,
            up_weight,
            gate_weight,
            saved_gate[0],
            saved_up[0],
        )
    )
    grad_up, grad_gate, grad_down = pl.pallas_call(
        grads_kernel,
        out_shape=[shape((WIDTH, units), BF16)] * 3,
        in_specs=[smem] + [vmem] * 3,
        out_specs=[vmem] * 3,
        scratch_shapes=[pltpu.VMEM((3, OWN, WIDTH, BLOCK), F32)],
        compiler_params=pltpu.CompilerParams(vmem_limit_bytes=VMEM_LIMIT),
    )(places, pairs, go, inp)
    return (grad_x.T, grad_up, grad_gate, grad_down.T)


def solution(mesh):
    side = 1
    while 2 * side * side < mesh.shape["dp"]:
        side += 1
    in_specs = (
        P(None, "dp"),
        P(None, "dp"),
        P("dp", "blk"),
        P("dp", "blk"),
        P("blk", "dp"),
        P("blk", None, None, None),
        P("blk", None, None, None),
        P(),
        P(),
    )
    out_specs = (P("blk", "dp"), P("dp", "blk"), P("dp", "blk"), P("blk", "dp"))
    return jax.shard_map(
        functools.partial(shards, side, mesh.shape["blk"]),
        mesh=mesh,
        in_specs=in_specs,
        out_specs=out_specs,
        check_vma=False,
    )
```

```python
import functools

import jax
import jax.numpy as jnp
from jax import lax
from jax.experimental import pallas as pl
from jax.experimental.pallas import tpu as pltpu
from jax.sharding import PartitionSpec as P

MESH = pl.DeviceIdType.MESH
BF16 = jnp.bfloat16
F32 = jnp.float32

WIDTH = 64
TILES = 10
TILE = 128
BLOCK = 128
KMAX = 24
PER = 3
PAIRS = TILES * PER
OWN = 28
HALF_PAIRS = PAIRS // 2
HALF_TILES = TILES // 2
HALF = HALF_PAIRS * TILE
PART_ROWS = WIDTH + 16
VMEM_LIMIT = 24 * 1024 * 1024


EARLY = 1
SUBS = 2


def sizes(side):
    chunk = HALF // side
    subs = []
    offset = 0
    for n in range(SUBS):
        number = min(-(-chunk // (SUBS * 16 * side)) * 16 * side, chunk - offset)
        piece = -(-number // side // 16) * 16
        subs.append((offset, number, piece))
        offset += number
    return chunk, subs


def stride_of(side):
    return sum(piece for _, _, piece in sizes(side)[1]) * side


def rows_of(ref, half, place, chunk, stride):
    first = place * TILE
    parts = []
    left = TILE
    while left:
        number, offset = divmod(first, chunk)
        take = min(left, chunk - offset)
        start = number * stride + offset
        parts.append(ref[half, start : start + take, :])
        first += take
        left -= take
    return parts[0] if len(parts) == 1 else jnp.concatenate(parts, axis=0)


def sum_kernel(
    side,
    depth,
    ids,
    counts,
    go_hbm,
    down_hbm,
    inp_hbm,
    up_hbm,
    gate_hbm,
    sg_hbm,
    su_hbm,
    places,
    gx_out,
    pairs,
    go,
    inp,
    up,
    gate,
    sg,
    su,
    gh,
    weights,
    gx,
    z_send,
    z_recv,
    down,
    picked,
    own,
    half_send,
    half_recv,
    a_send,
    a_recv,
    b_send,
    b_recv,
    load_sem,
    h_ssem,
    h_rsem,
    a_ssem,
    a_rsem,
    b_ssem,
    b_rsem,
    c_ssem,
    c_rsem,
    d_ssem,
    d_rsem,
    f_ssem,
    f_rsem,
    z_ssem,
    z_rsem,
):
    chunk, subs = sizes(side)
    stride = stride_of(side)
    dp = lax.axis_index("dp")
    me_z = lax.axis_index("blk")
    core = dp % 2
    me_y = (dp // 2) % side
    me_x = dp // (2 * side)
    partner = dp + 1 - 2 * core
    me_a = me_x + core * (me_y - me_x)
    me_b = me_y + core * (me_x - me_y)
    step_a = (1 - core) * 2 * side + core * 2
    step_b = (1 - core) * 2 + core * 2 * side

    def along_a(i):
        return dp + (i - me_a) * step_a

    def along_b(i):
        return dp + (i - me_b) * step_b

    def other(me, d):
        return (me + d) % side

    barrier = pltpu.get_barrier_semaphore()
    pl.semaphore_signal(barrier, inc=1, device_id=(partner, me_z), device_id_type=MESH)
    for d in range(1, side):
        pl.semaphore_signal(
            barrier, inc=1, device_id=(along_a(other(me_a, d)), me_z), device_id_type=MESH
        )
        pl.semaphore_signal(
            barrier, inc=1, device_id=(along_b(other(me_b, d)), me_z), device_id_type=MESH
        )

    for d in range(1, depth):
        pl.semaphore_signal(
            barrier, inc=1, device_id=(dp, (me_z + d) % depth), device_id_type=MESH
        )

    loads = [
        pltpu.make_async_copy(source, target, load_sem.at[i])
        for i, (source, target) in enumerate(
            (
                (down_hbm, down),
                (go_hbm, go),
                (inp_hbm, inp),
                (up_hbm, up),
                (gate_hbm, gate),
                (sg_hbm, sg),
                (su_hbm, su),
            )
        )
    ]
    for load in loads:
        load.start()

    low = me_z * OWN

    first = jnp.int32(0)
    for t in range(TILES):
        live = counts[t]
        packed = jnp.int32(0)
        shift = jnp.int32(0)
        for k in range(KMAX):
            block = ids[t, k] - low
            owned = (block >= 0) & (block < OWN) & (live > k)
            packed = packed + jnp.where(owned, lax.shift_left(block + 1, shift), 0)
            shift = shift + jnp.where(owned, 5, 0)
        number = jnp.int32(0)
        for j in range(PER):
            place = lax.shift_right_logical(packed, jnp.int32(5 * j)) & 31
            places[t * PER + j] = place
            places[PAIRS + t * PER + j] = jnp.minimum(first + j, PAIRS - 1)
            number = number + jnp.where(place > 0, 1, 0)
        first = first + number

    loads[0].wait()
    for t in range(TILES):
        wanted = [places[t * PER + j] for j in range(PER)]
        found = [down[:, 0:BLOCK]] * PER
        for b in range(1, OWN):
            block = down[:, b * BLOCK : (b + 1) * BLOCK]
            found = [jnp.where(w == b + 1, block, f) for w, f in zip(wanted, found)]
        for j in range(PER):
            picked[t, :, j * BLOCK : (j + 1) * BLOCK] = found[j]
    loads[1].wait()

    def hidden_terms(t):
        tokens = go[:, pl.ds(pl.multiple_of(t * TILE, TILE), TILE)]
        return lax.dot_general(
            tokens, picked[t], (((0,), (0,)), ((), ())), preferred_element_type=F32
        )

    def h_copy(i):
        rows = pl.ds(i * PER * TILE, PER * TILE)
        return pltpu.make_async_remote_copy(
            src_ref=half_send.at[rows],
            dst_ref=half_recv.at[rows],
            send_sem=h_ssem.at[i],
            recv_sem=h_rsem.at[i],
            device_id=(partner, me_z),
            device_id_type=MESH,
        )

    for i in range(HALF_TILES):
        others = hidden_terms((1 - core) * HALF_TILES + i)
        for j in range(PER):
            start = (i * PER + j) * TILE
            half_send[start : start + TILE, :] = others[:, j * BLOCK : (j + 1) * BLOCK].astype(BF16)
    for i in range(HALF_TILES):
        mine = hidden_terms(core * HALF_TILES + i)
        for j in range(PER):
            start = (i * PER + j) * TILE
            own[start : start + TILE, :] = mine[:, j * BLOCK : (j + 1) * BLOCK]
        if i == EARLY:
            pl.semaphore_wait(barrier, 1 + 2 * (side - 1) + depth - 1)
            for k in range(HALF_TILES):
                h_copy(k).start()
    for i in range(HALF_TILES):
        h_copy(i).wait_recv()
        rows = slice(i * PER * TILE, (i + 1) * PER * TILE)
        a_send[rows, :] = (own[rows, :] + half_recv[rows, :].astype(F32)).astype(BF16)

    def a_copy(to, slot, n):
        offset, number, _ = subs[n]
        rows = pl.ds(pl.multiple_of(to * chunk + offset, 16), number)
        return pltpu.make_async_remote_copy(
            src_ref=a_send.at[rows],
            dst_ref=a_recv.at[slot, offset : offset + number],
            send_sem=a_ssem.at[n, to],
            recv_sem=a_rsem.at[n, slot],
            device_id=(along_a(to), me_z),
            device_id_type=MESH,
        )

    def b_copy(to, slot, n):
        offset, _, piece = subs[n]
        rows = pl.ds(pl.multiple_of(offset + to * piece, 16), piece)
        return pltpu.make_async_remote_copy(
            src_ref=b_send.at[rows],
            dst_ref=b_recv.at[n, slot, 0:piece],
            send_sem=b_ssem.at[n, to],
            recv_sem=b_rsem.at[n, slot],
            device_id=(along_b(to), me_z),
            device_id_type=MESH,
        )

    def c_copy(to, slot, n):
        offset, _, piece = subs[n]
        rows = pl.ds(pl.multiple_of(me_a * stride + offset + slot * piece, 16), piece)
        return pltpu.make_async_remote_copy(
            src_ref=gh.at[core, rows],
            dst_ref=gh.at[core, rows],
            send_sem=c_ssem.at[n, to],
            recv_sem=c_rsem.at[n, slot],
            device_id=(along_b(to), me_z),
            device_id_type=MESH,
        )

    def d_copy(to, slot, n):
        offset, number, _ = subs[n]
        rows = pl.ds(pl.multiple_of(slot * stride + offset, 16), number)
        return pltpu.make_async_remote_copy(
            src_ref=gh.at[core, rows],
            dst_ref=gh.at[core, rows],
            send_sem=d_ssem.at[n, to],
            recv_sem=d_rsem.at[n, slot],
            device_id=(along_a(to), me_z),
            device_id_type=MESH,
        )

    def f_copy(slot, half, n):
        offset, number, _ = subs[n]
        rows = pl.ds(pl.multiple_of(slot * stride + offset, 16), number)
        return pltpu.make_async_remote_copy(
            src_ref=gh.at[half, rows],
            dst_ref=gh.at[half, rows],
            send_sem=f_ssem.at[n, slot],
            recv_sem=f_rsem.at[n, slot],
            device_id=(partner, me_z),
            device_id_type=MESH,
        )

    order = sorted(range(1, side), key=lambda d: -min(d, side - d))
    steps = range(len(subs))
    for n in steps:
        for d in order:
            a_copy(other(me_a, d), me_a, n).start()

    loads[5].wait()
    loads[6].wait()
    for number in range(PAIRS):
        t, j = divmod(number, PER)
        slot = places[PAIRS + number]
        live = jnp.where(places[number] > 0, jnp.float32(1), jnp.float32(0))
        gate_value = sg[j]
        up_value = su[j]
        for c in range(j + 1, min(t * PER + j, PAIRS - 1) + 1):
            gate_value = jnp.where(slot == c, sg[c], gate_value)
            up_value = jnp.where(slot == c, su[c], up_value)
        gate_value = gate_value.astype(F32)
        up_value = up_value.astype(F32)
        positive = jnp.maximum(gate_value, 0.0) * live
        pairs[number, :, 0:BLOCK] = positive.astype(BF16)
        pairs[number, :, BLOCK : 2 * BLOCK] = (
            jnp.where(gate_value > 0, up_value, 0.0) * live
        ).astype(BF16)
        pairs[number, :, 2 * BLOCK : 3 * BLOCK] = (positive * up_value).astype(BF16)

    for n in steps:
        offset, number, piece = subs[n]
        rows = pl.ds(pl.multiple_of(me_a * chunk + offset, 16), number)
        total = a_send[rows, :].astype(F32)
        for d in reversed(order):
            source = other(me_a, d)
            a_copy(source, source, n).wait_recv()
            total = total + a_recv[source, offset : offset + number, :].astype(F32)
        b_send[offset : offset + number, :] = total.astype(BF16)
        end = offset + piece * side
        if end > offset + number:
            b_send[offset + number : end, :] = jnp.zeros((end - offset - number, BLOCK), BF16)
        for d in order:
            b_copy(other(me_b, d), me_b, n).start()
    for n in steps:
        offset, _, piece = subs[n]
        total = b_send[pl.ds(pl.multiple_of(offset + me_b * piece, 16), piece), :].astype(F32)
        for d in reversed(order):
            source = other(me_b, d)
            b_copy(source, source, n).wait_recv()
            total = total + b_recv[n, source, 0:piece, :].astype(F32)
        rows = pl.ds(pl.multiple_of(me_a * stride + offset + me_b * piece, 16), piece)
        gh[core, rows, :] = total.astype(BF16)
        for d in order:
            c_copy(other(me_b, d), me_b, n).start()
    for n in steps:
        for d in reversed(order):
            source = other(me_b, d)
            c_copy(source, source, n).wait_recv()
        for d in order:
            d_copy(other(me_a, d), me_a, n).start()
        f_copy(me_a, core, n).start()

    loads[3].wait()
    loads[4].wait()
    for t in range(TILES):
        wanted = [places[t * PER + j] for j in range(PER)]
        for k, source in enumerate((up, gate)):
            found = [source[:, 0:BLOCK]] * PER
            for b in range(1, OWN):
                block = source[:, b * BLOCK : (b + 1) * BLOCK]
                found = [jnp.where(w == b + 1, block, f) for w, f in zip(wanted, found)]
            for j in range(PER):
                weights[t, :, (2 * j + k) * BLOCK : (2 * j + k + 1) * BLOCK] = found[j]

    for n in steps:
        for d in reversed(order):
            source = other(me_a, d)
            d_copy(source, source, n).wait_recv()
            f_copy(source, core, n).start()
    for part in range(2 * HALF_TILES):
        if part == HALF_TILES:
            for n in steps:
                for d in range(side):
                    f_copy(d, 1 - core, n).wait_recv()
        i = part % HALF_TILES
        half = core if part < HALF_TILES else 1 - core
        t = half * HALF_TILES + i
        values = []
        for j in range(PER):
            number = t * PER + j
            value = rows_of(gh, half, i * PER + j, chunk, stride).astype(F32)
            for k in range(2):
                lanes = slice(k * BLOCK, (k + 1) * BLOCK)
                grad = (value * pairs[number, :, lanes].astype(F32)).astype(BF16)
                pairs[number, :, lanes] = grad
                values.append(grad)
        gx[t] = lax.dot_general(
            weights[t],
            jnp.concatenate(values, axis=1),
            (((1,), (1,)), ((), ())),
            preferred_element_type=F32,
        )

    lanes = lax.broadcasted_iota(jnp.int32, (WIDTH, TILE), 1)
    short = lax.broadcasted_iota(jnp.int32, (16, TILE), 1)
    for to in range(depth):
        q, o = divmod(to * TILES * TILE // depth, TILE)
        after = gx[q + 1]
        if o:
            first = jnp.where(
                lanes < TILE - o,
                pltpu.roll(gx[q], TILE - o, 1),
                pltpu.roll(after, TILE - o, 1),
            )
        else:
            first = gx[q]
        z_send[to, 0:WIDTH, :] = first.astype(BF16)
        rest = jnp.zeros((16, TILE), F32)
        for s in range(4):
            shift = (32 * s - o) % TILE
            moved = after[16 * s : 16 * (s + 1), :]
            if shift:
                moved = pltpu.roll(moved, shift, 1)
            rest = jnp.where(short // 32 == s, moved, rest)
        z_send[to, WIDTH:PART_ROWS, :] = rest.astype(BF16)

    def z_copy(to, slot):
        return pltpu.make_async_remote_copy(
            src_ref=z_send.at[to],
            dst_ref=z_recv.at[slot],
            send_sem=z_ssem.at[to],
            recv_sem=z_rsem.at[slot],
            device_id=(dp, to),
            device_id_type=MESH,
        )

    z_order = sorted(range(1, depth), key=lambda d: -min(d, depth - d))
    for d in z_order:
        z_copy((me_z + d) % depth, me_z).start()
    total = z_send[me_z].astype(F32)
    for d in reversed(z_order):
        source = (me_z + d) % depth
        z_copy(source, source).wait_recv()
        total = total + z_recv[source].astype(F32)
    gx_out[:, 0:TILE] = total[0:WIDTH, :].astype(BF16)
    rest = total[WIDTH:PART_ROWS, :]
    for s in range(4):
        moved = pltpu.roll(rest, TILE - 32 * s, 1) if s else rest
        gx_out[16 * s : 16 * (s + 1), TILE : TILE + 32] = moved[:, 0:32].astype(BF16)
    for d in range(1, depth):
        z_copy((me_z + d) % depth, me_z).wait_send()

    loads[2].wait()
    for i in range(HALF_TILES):
        h_copy(i).wait_send()
    for n in steps:
        for d in range(1, side):
            a_copy(other(me_a, d), me_a, n).wait_send()
            b_copy(other(me_b, d), me_b, n).wait_send()
            c_copy(other(me_b, d), me_b, n).wait_send()
            d_copy(other(me_a, d), me_a, n).wait_send()
        for d in range(side):
            f_copy(d, core, n).wait_send()


def grads_kernel(places, pairs, go, inp, up_out, gate_out, down_out, totals):
    totals[...] = jnp.zeros_like(totals)
    for number in range(PAIRS):
        t = number // PER
        tokens = slice(t * TILE, (t + 1) * TILE)
        block = jnp.maximum(places[number] - 1, 0)
        pair = jnp.dot(
            inp[:, tokens], pairs[number, :, 0 : 2 * BLOCK], preferred_element_type=F32
        )
        totals[0, block] += pair[:, 0:BLOCK]
        totals[1, block] += pair[:, BLOCK : 2 * BLOCK]
        totals[2, block] += jnp.dot(
            go[:, tokens], pairs[number, :, 2 * BLOCK : 3 * BLOCK], preferred_element_type=F32
        )
    for i, out in enumerate((up_out, gate_out, down_out)):
        for b in range(OWN):
            out[:, b * BLOCK : (b + 1) * BLOCK] = totals[i, b].astype(BF16)


def in_hbm(*arrays):
    return [pltpu.with_memory_space_constraint(array, pltpu.HBM) for array in arrays]


def shards(
    side,
    depth,
    inputs,
    grad_out,
    up_weight,
    gate_weight,
    down_weight,
    saved_gate,
    saved_up,
    block_ids,
    counts,
):
    tokens = TILES * TILE
    units = OWN * BLOCK
    chunk, subs = sizes(side)
    piece = max(piece for _, _, piece in subs)
    stride = stride_of(side)
    dma = pltpu.SemaphoreType.DMA
    anywhere = pl.BlockSpec(memory_space=pl.ANY)
    smem = pl.BlockSpec(memory_space=pltpu.SMEM)
    vmem = pl.BlockSpec(memory_space=pltpu.VMEM)
    shape = jax.ShapeDtypeStruct
    places, grad_x, pairs, go, inp = pl.pallas_call(
        functools.partial(sum_kernel, side, depth),
        out_shape=[
            shape((2 * PAIRS,), jnp.int32),
            shape((WIDTH, tokens // depth), BF16),
            shape((PAIRS, TILE, 3 * BLOCK), BF16),
            shape((WIDTH, tokens), BF16),
            shape((WIDTH, tokens), BF16),
        ],
        in_specs=[smem] * 2 + [anywhere] * 7,
        out_specs=[smem] + [vmem] * 4,
        scratch_shapes=[
            pltpu.VMEM((WIDTH, units), BF16),
            pltpu.VMEM((WIDTH, units), BF16),
            pltpu.VMEM((PAIRS, TILE, BLOCK), BF16),
            pltpu.VMEM((PAIRS, TILE, BLOCK), BF16),
            pltpu.VMEM((2, side * stride, BLOCK), BF16),
            pltpu.VMEM((TILES, WIDTH, 2 * PER * BLOCK), BF16),
            pltpu.VMEM((TILES, WIDTH, TILE), F32),
            pltpu.VMEM((depth, PART_ROWS, TILE), BF16),
            pltpu.VMEM((depth, PART_ROWS, TILE), BF16),
            pltpu.VMEM((WIDTH, units), BF16),
            pltpu.VMEM((TILES, WIDTH, PER * BLOCK), BF16),
            pltpu.VMEM((HALF, BLOCK), F32),
            pltpu.VMEM((HALF, BLOCK), BF16),
            pltpu.VMEM((HALF, BLOCK), BF16),
            pltpu.VMEM((HALF, BLOCK), BF16),
            pltpu.VMEM((side, chunk, BLOCK), BF16),
            pltpu.VMEM((stride, BLOCK), BF16),
            pltpu.VMEM((SUBS, side, piece, BLOCK), BF16),
            dma((7,)),
            dma((HALF_TILES,)),
            dma((HALF_TILES,)),
        ]
        + [dma((SUBS, side))] * 10
        + [dma((depth,))] * 2,
        compiler_params=pltpu.CompilerParams(
            collective_id=0, has_side_effects=True, vmem_limit_bytes=VMEM_LIMIT
        ),
    )(
        *in_hbm(
            block_ids,
            counts,
            grad_out.T,
            down_weight.T,
            inputs.T,
            up_weight,
            gate_weight,
            saved_gate[0],
            saved_up[0],
        )
    )
    grad_up, grad_gate, grad_down = pl.pallas_call(
        grads_kernel,
        out_shape=[shape((WIDTH, units), BF16)] * 3,
        in_specs=[smem] + [vmem] * 3,
        out_specs=[vmem] * 3,
        scratch_shapes=[pltpu.VMEM((3, OWN, WIDTH, BLOCK), F32)],
        compiler_params=pltpu.CompilerParams(vmem_limit_bytes=VMEM_LIMIT),
    )(places, pairs, go, inp)
    return (grad_x.T, grad_up, grad_gate, grad_down.T)


def solution(mesh):
    side = 1
    while 2 * side * side < mesh.shape["dp"]:
        side += 1
    in_specs = (
        P(None, "dp"),
        P(None, "dp"),
        P("dp", "blk"),
        P("dp", "blk"),
        P("blk", "dp"),
        P("blk", None, None, None),
        P("blk", None, None, None),
        P(),
        P(),
    )
    out_specs = (P("blk", "dp"), P("dp", "blk"), P("dp", "blk"), P("blk", "dp"))
    return jax.shard_map(
        functools.partial(shards, side, mesh.shape["blk"]),
        mesh=mesh,
        in_specs=in_specs,
        out_specs=out_specs,
        check_vma=False,
    )
```
